32 devices in a mesh: grp: 2 (over y), pair: 4 (over z), rep: 2 (over x), sub: 2 (over core).
Axes of the slice: x: 2, y: 2, z: 4, core: 2. Of those that a mesh axis runs over, the one named last changes fastest.
Arguments:
- cholesky: bfloat16 [256, 640, 640], P('sub', 'pair'), may hold values from -0.015625 to 0.015625
- trial_orbitals: bfloat16 [640, 192], replicated, may hold values from -0.25 to 0.25
- walkers: bfloat16 [32, 640, 192], P(('grp', 'pair', 'rep'), None, 'sub'), parts along dimension 0, may hold values from -6 to 6
- intersection_inverse: bfloat16 [32, 192, 192], P(('grp', 'pair', 'rep')), parts along dimension 0, may hold values from -0.4375 to 0.4375
- noise_stream: float32 [2048], P('grp'), parts along dimension 0, may hold values from -6 to 6
- offsets: int32 [32], P('grp'), parts along dimension 0, may hold values from 0 to 768
- parents: int32 [32], P(('grp', 'pair', 'rep')), parts along dimension 0, may hold values from 0 to 7
Outputs:
- new_walkers: bfloat16 [32, 640, 192], P(('grp', 'pair', 'rep'), None, 'sub'), parts along dimension 0
- force_bias: float32 [32, 256], P(('grp', 'pair', 'rep'), 'sub'), parts along dimension 0
The draws below stay inside these ranges and needn't reach their ends.
There are 2 independent parts, one for each index of `grp`. The reference program is written for one: setup_inputs(seed, part) draws one part's arguments, and reference() takes and returns one part's arrays. A program takes and returns all parts, laid end to end along the dimension named above; an argument that names none is the same for every part. Nothing has to cross between parts.
All inputs are finite; a program needn't handle non-finite values.
Results may differ from the reference program's by a relative error of at most 0.035.
Values may be sent and summed in bfloat16 or wider, within the bound.
A program may use at most 64 MiB of HBM per device.

```python
import math
import jax
import jax.numpy as jnp
import numpy as np

M = 640
NEL = 192
NCHOL = 256
TAYLOR = 6
WALK_DEV = 2
W = 16
NSTREAM = 1024
N_PAIR = 4
N_REP = 2


def with_ends(drawn, stream_key, low, top_value):
    dims = drawn.shape
    spot = [jax.random.randint(jax.random.fold_in(stream_key, axis), (), 0, dims[axis]) for axis in range(len(dims))]
    drawn = drawn.at[tuple(spot)].set(low)
    longest = dims.index(max(dims))
    spot[longest] = (spot[longest] + 1) % dims[longest]
    return drawn.at[tuple(spot)].set(top_value)


def shard_levels(own_key, dims, split, least, high):
    loudness, own = 1.0, jax.random.fold_in(own_key, 6)
    for position, shards_of in split:
        draws = jnp.exp(jax.random.uniform(jax.random.fold_in(own, position), (shards_of,), jnp.float32, least / len(split), high / len(split)))
        loudness = loudness * jnp.repeat(draws, dims[position] // shards_of).reshape([-1 if axis == position else 1 for axis in range(len(dims))])
    return loudness


def cumulative_ranks(count, lean):
    loads = [(1 << 20) // math.isqrt(standing ** lean) + 1 for standing in range(1, count + 1)]
    deviation = 1 + sum(loads) // (1 << 30)
    return np.cumsum(np.array([max(1, weight // deviation) for weight in loads]))


def ranked(stream_key, shape, number_of, slope):
    grid = cumulative_ranks(number_of, slope)
    lot = jax.random.randint(jax.random.fold_in(stream_key, 1), shape, 0, int(grid[number_of - 1]))
    standing = jnp.searchsorted(jnp.asarray(grid, jnp.int32), lot, side="right")
    return jax.random.permutation(jax.random.fold_in(stream_key, 2), number_of)[standing].astype(jnp.int32)


def gaussian(rng, dims, width, limit, shards=(), kind=jnp.bfloat16):
    array = width * jax.random.normal(rng, dims, jnp.float32)
    if shards:
        array = array * shard_levels(rng, dims, shards, -0.22, 0.18)
    return jnp.clip(array, -limit, limit).astype(kind)


def setup_inputs(seed: int = 0, part: int = 0) -> dict:
    key_of = jax.random.split(jax.random.key(seed), 8)
    part_splits = jax.random.split(jax.random.fold_in(key_of[7], part), 8)
    return {
        "cholesky": gaussian(key_of[0], (NCHOL, M, M), (M * NEL) ** -0.5, 0.015625, ((0, 2), (1, 4))),
        "trial_orbitals": gaussian(key_of[1], (M, NEL), M ** -0.5, 0.25),
        "walkers": gaussian(part_splits[2], (W, M, NEL), 1.0, 6.0, ((0, 8), (2, 2))),
        "intersection_inverse": gaussian(part_splits[3], (W, NEL, NEL), NEL ** -0.5, 0.4375, ((0, 8),)),
        "noise_stream": gaussian(part_splits[4], (NSTREAM,), 1.0, 6.0, (), jnp.float32),
        "offsets": with_ends(jax.random.randint(part_splits[5], (W,), 0, NSTREAM - NCHOL + 1), jax.random.fold_in(part_splits[5], 1), 0, NSTREAM - NCHOL).astype(jnp.int32),
        "parents": with_ends(ranked(part_splits[6], (W,), N_PAIR * WALK_DEV, 2), jax.random.fold_in(part_splits[6], 3), 0, (N_PAIR * WALK_DEV) - 1).astype(jnp.int32),
    }


field_scale = 1.6


def reference(cholesky, trial_orbitals, walkers, intersection_inverse, noise_stream, offsets, parents):
    chol_wide = cholesky.astype(jnp.float32)
    half_rotated = jnp.einsum('gpq,qi->gpi', chol_wide, trial_orbitals.astype(jnp.float32)).astype(jnp.bfloat16)
    mixed = jnp.einsum('wpj,wji->wpi', walkers.astype(jnp.float32), intersection_inverse.astype(jnp.float32)).astype(jnp.bfloat16)
    force_bias = jnp.einsum('wpi,gpi->wg', mixed.astype(jnp.float32), half_rotated.astype(jnp.float32))
    window_index = offsets[:, None] + jnp.arange(NCHOL, dtype=jnp.int32)[None, :]
    fields = (noise_stream[window_index] - force_bias).astype(jnp.bfloat16)
    potential = (field_scale * jnp.einsum('wg,gpq->wpq', fields.astype(jnp.float32), chol_wide)).astype(jnp.bfloat16)
    potential_wide = potential.astype(jnp.float32)
    taylor_term = walkers
    summed = walkers.astype(jnp.float32)
    for degree in range(1, TAYLOR + 1):
        product = jnp.einsum('wpq,wqi->wpi', potential_wide, taylor_term.astype(jnp.float32))
        taylor_term = (product / jnp.float32(degree)).astype(jnp.bfloat16)
        summed = summed + taylor_term.astype(jnp.float32)
    propagated = summed.astype(jnp.bfloat16)
    row_walkers = propagated.reshape(N_PAIR, N_REP, WALK_DEV, M, NEL)
    row_walkers = jnp.transpose(row_walkers, (1, 0, 2, 3, 4)).reshape(N_REP, N_PAIR * WALK_DEV, M, NEL)
    parent_grid = parents.reshape(N_PAIR, N_REP, WALK_DEV)
    row_numbers = jnp.arange(N_REP, dtype=jnp.int32)[None, :, None]
    new_walkers = row_walkers[row_numbers, parent_grid].reshape(W, M, NEL)
    return new_walkers, force_bias
```

```python
import functools

import jax
import jax.numpy as jnp
from jax import lax
from jax.experimental import pallas as pl
from jax.experimental.pallas import tpu as pltpu
from jax.sharding import PartitionSpec as P

TAYLOR = 6
GROUP = 16
LANES = 128

field_scale = 1.6

MESH = pl.DeviceIdType.MESH
F32 = jnp.float32
BF16 = jnp.bfloat16
NT = (((1,), (1,)), ((), ()))


def step_kernel(
    n, chol, trial, walk, inverse, halves, drawn, picks,
    pot_out, halves_out, bias_out,
    cbuf, mixed, mixbuf, rbuf, ybuf, ebuf, fbsend, fbbuf, fpad, kron, tmp, keep, psend, precv, pfin,
    csem, msem, ssem, hsem, rsem, fsem, qsem, psem, osem,
):
    a = lax.axis_index("pair")
    s = lax.axis_index("sub")
    groups, count = cbuf.shape[0], cbuf.shape[1]
    orbitals = chol.shape[2]
    electrons = walk.shape[2]
    walks = 2 * n
    wide = walks * GROUP
    deep = count * GROUP

    def chol_copy(j):
        return pltpu.make_async_copy(
            chol.at[:, pl.ds(pl.multiple_of(j * GROUP, GROUP), GROUP), :], cbuf.at[j], csem.at[j]
        )

    @pl.loop(0, groups)
    def _(j):
        chol_copy(j).start()

    peers = [(d, lax.rem(a + d, n)) for d in range(1, n)]

    def remote(src, dst, sems, d, target):
        return pltpu.make_async_remote_copy(
            src_ref=src, dst_ref=dst, send_sem=sems.at[0, d], recv_sem=sems.at[1, d],
            device_id=target, device_id_type=MESH,
        )

    barrier = pltpu.get_barrier_semaphore()
    pl.semaphore_signal(barrier, inc=1, device_id={"sub": 1 - s}, device_id_type=MESH)
    for _, b in peers:
        pl.semaphore_signal(barrier, inc=1, device_id={"pair": b}, device_id_type=MESH)

    own_halves = pltpu.make_async_copy(halves, halves_out.at[a], osem.at[0])
    own_halves.start()
    for b in range(n):
        mixed[b] = jnp.dot(walk[b], inverse[...], preferred_element_type=F32).astype(BF16)
    mixbuf[s, a] = mixed[a]
    rbuf[:, a] = picks[...]
    pl.semaphore_wait(barrier, n)

    mixed_copies = [remote(mixed.at[b], mixbuf.at[s, a], msem, d, {"pair": b}) for d, b in peers]
    pick_copies = [remote(picks, rbuf.at[:, a], rsem, d, {"pair": b}) for d, b in peers]
    half_copies = [remote(halves, halves_out.at[a], hsem, d, {"pair": b}) for d, b in peers]
    for copy in mixed_copies + pick_copies:
        copy.start()

    ybuf[...] = jnp.zeros_like(ybuf)
    fpad[...] = jnp.zeros_like(fpad)
    ebuf[...] = jnp.where(
        lax.broadcasted_iota(jnp.int32, (count, deep), 1) // GROUP
        == lax.broadcasted_iota(jnp.int32, (count, deep), 0), 1.0, 0.0
    ).astype(BF16)

    for copy in mixed_copies:
        copy.wait_recv()
    across = remote(mixbuf.at[s], mixbuf.at[s], ssem, 0, {"sub": 1 - s})
    across.start()
    for copy in half_copies:
        copy.start()
    across.wait_recv()

    tile = max(GROUP, min(deep, 65536 // wide) // GROUP * GROUP)

    @pl.loop(0, groups)
    def _(j):
        chol_copy(j).wait()
        rows = mixbuf[:, :, pl.ds(pl.multiple_of(j * GROUP, GROUP), GROUP), :]
        density = lax.dot_general(
            rows.reshape(wide, electrons), trial[...], NT, preferred_element_type=F32
        ).astype(BF16)
        part = tile // GROUP

        @pl.loop(0, deep // tile)
        def _(t):
            block = cbuf[j, pl.ds(t * part, part)].reshape(tile, orbitals)
            at = pl.ds(pl.multiple_of(t * tile, tile), tile)
            ybuf[at, :] += lax.dot_general(block, density, NT, preferred_element_type=F32)

    same = (
        lax.broadcasted_iota(jnp.int32, (1, GROUP, wide), 1)
        == lax.broadcasted_iota(jnp.int32, (1, GROUP, wide), 2) % GROUP
    )
    traced = jnp.sum(jnp.where(same, ybuf[...].reshape(count, GROUP, wide), 0.0), axis=1)
    adder = jnp.where(
        lax.broadcasted_iota(jnp.int32, (walks, wide), 1) // GROUP
        == lax.broadcasted_iota(jnp.int32, (walks, wide), 0), 1.0, 0.0
    )
    partial = lax.dot_general(
        adder, traced, NT, preferred_element_type=F32, precision=lax.Precision.HIGHEST
    )
    fbsend[...] = partial
    fbbuf[a] = partial
    bias_copies = [remote(fbsend, fbbuf.at[a], fsem, d, {"pair": b}) for d, b in peers]
    for copy in bias_copies:
        copy.start()
    for copy in bias_copies + pick_copies:
        copy.wait_recv()
    total = jnp.sum(fbbuf[...], axis=0)
    bias_out[...] = total
    fpad[0:walks, :] = drawn[...] - total
    fields = fpad[...].astype(BF16)

    step = 8 * GROUP
    chunks = wide // step

    @pl.loop(0, chunks)
    def _(c):
        chosen = rbuf[...].reshape(chunks, step, LANES) if chunks == 1 else None
        if chunks == 1:
            chosen = chosen[0]
        else:
            per = n // 8
            chosen = rbuf[c // per, pl.ds(lax.rem(c, per) * 8, 8)].reshape(step, LANES)
        spread = jnp.dot(chosen, fields, preferred_element_type=F32).astype(BF16)
        full = jnp.dot(spread, ebuf[...], preferred_element_type=F32)
        diagonal = (
            lax.broadcasted_iota(jnp.int32, (step, deep), 0) % GROUP
            == lax.broadcasted_iota(jnp.int32, (step, deep), 1) % GROUP
        )
        kron[c] = jnp.where(diagonal, full, 0.0).astype(BF16)

    def part_copy(j):
        return pltpu.make_async_remote_copy(
            src_ref=psend.at[j], dst_ref=precv.at[j], send_sem=qsem.at[0, j], recv_sem=qsem.at[1, j],
            device_id={"sub": 1 - s}, device_id_type=MESH,
        )

    def pot_copy(d, b, j):
        at = pl.ds(pl.multiple_of(j * GROUP, GROUP), GROUP)
        return pltpu.make_async_remote_copy(
            src_ref=pfin.at[b, at], dst_ref=pot_out.at[a, at],
            send_sem=psem.at[0, d, j], recv_sem=psem.at[1, d, j],
            device_id={"pair": b}, device_id_type=MESH,
        )

    def finish(j):
        part_copy(j).wait_recv()
        at = pl.ds(pl.multiple_of(j * GROUP, GROUP), GROUP)
        pfin[:, at, :] = (field_scale * (keep[j] + precv[j].astype(F32))).astype(BF16)
        for d, b in peers:
            pot_copy(d, b, j).start()

    @pl.loop(0, groups)
    def _(j):
        @pl.loop(0, chunks)
        def _(c):
            tmp[pl.ds(c * 8, 8)] = jnp.dot(
                kron[c], cbuf[j].reshape(deep, orbitals), preferred_element_type=F32
            ).reshape(8, GROUP, orbitals)

        psend[j] = tmp[pl.ds((1 - s) * n, n)].astype(BF16)
        part_copy(j).start()
        keep[j] = tmp[pl.ds(s * n, n)]

        @pl.when(j > 0)
        def _():
            finish(j - 1)

    finish(groups - 1)
    own_pot = pltpu.make_async_copy(pfin.at[a], pot_out.at[a], osem.at[1])
    own_pot.start()
    across.wait_send()
    for copy in mixed_copies + pick_copies + bias_copies:
        copy.wait_send()
    for copy in half_copies:
        copy.wait()
    own_halves.wait()

    @pl.loop(0, groups)
    def _(j):
        part_copy(j).wait_send()
        for d, b in peers:
            pot_copy(d, b, j).wait()

    own_pot.wait()


def shards(cholesky, trial_orbitals, walkers, intersection_inverse, noise_stream, offsets, parents):
    count, rows, orbitals = cholesky.shape
    walk_count, _, half = walkers.shape
    electrons = trial_orbitals.shape[1]
    n = lax.axis_size("pair")
    rep_size = lax.axis_size("rep")
    pair_index = lax.axis_index("pair")
    rep_index = lax.axis_index("rep")
    sub_index = lax.axis_index("sub")
    assert walk_count == 2 and lax.axis_size("sub") == 2
    padded = -(-rows // GROUP) * GROUP
    groups = padded // GROUP
    walks = walk_count * n
    wide, deep = walks * GROUP, count * GROUP
    if padded != rows:
        cholesky = jnp.pad(cholesky, ((0, 0), (0, padded - rows), (0, 0)))

    whole = lax.all_to_all(walkers, "sub", split_axis=0, concat_axis=2, tiled=True)
    blocks = whole.reshape(n, rows, electrons)
    if padded != rows:
        blocks = jnp.pad(blocks, ((0, 0), (0, padded - rows), (0, 0)))
    inverse = lax.dynamic_index_in_dim(intersection_inverse, sub_index, 0, False)

    offsets_grid = offsets.reshape(n, rep_size, walk_count)
    row_offsets = lax.dynamic_index_in_dim(offsets_grid, rep_index, 1, False).T.reshape(-1)
    wanted = row_offsets[:, None] + sub_index * count + jnp.arange(count, dtype=jnp.int32)[None, :]
    places = jnp.arange(noise_stream.shape[0], dtype=jnp.int32)
    drawn = jnp.sum(
        jnp.where(wanted[:, :, None] == places[None, None, :], noise_stream[None, None, :], 0.0), axis=2
    )

    columns = (parents % walk_count) * n + parents // walk_count
    picks = (columns[:, None] == jnp.arange(LANES, dtype=jnp.int32)[None, :]).astype(BF16)
    picks = jnp.broadcast_to(picks[:, None, :], (walk_count, GROUP, LANES))

    vmem = pl.BlockSpec(memory_space=pltpu.VMEM)
    hbm = pl.BlockSpec(memory_space=pl.ANY)
    dma = pltpu.SemaphoreType.DMA
    potential, gathered, bias = pl.pallas_call(
        functools.partial(step_kernel, n),
        out_shape=(
            jax.ShapeDtypeStruct((n, padded, orbitals), BF16),
            jax.ShapeDtypeStruct((n, walk_count, orbitals, half), BF16),
            jax.ShapeDtypeStruct((walks, count), F32),
        ),
        in_specs=[hbm, vmem, vmem, vmem, vmem, vmem, vmem],
        out_specs=(hbm, hbm, vmem),
        scratch_shapes=[
            pltpu.VMEM((groups, count, GROUP, orbitals), BF16),
            pltpu.VMEM((n, padded, electrons), BF16),
            pltpu.VMEM((2, n, padded, electrons), BF16),
            pltpu.VMEM((2, n, GROUP, LANES), BF16),
            pltpu.VMEM((deep, wide), F32),
            pltpu.VMEM((count, deep), BF16),
            pltpu.VMEM((walks, count), F32),
            pltpu.VMEM((n, walks, count), F32),
            pltpu.VMEM((LANES, count), F32),
            pltpu.VMEM((wide // (8 * GROUP), 8 * GROUP, deep), BF16),
            pltpu.VMEM((walks, GROUP, orbitals), F32),
            pltpu.VMEM((groups, n, GROUP, orbitals), F32),
            pltpu.VMEM((groups, n, GROUP, orbitals), BF16),
            pltpu.VMEM((groups, n, GROUP, orbitals), BF16),
            pltpu.VMEM((n, padded, orbitals), BF16),
            dma((groups,)),
            dma((2, n)),
            dma((2, 1)),
            dma((2, n)),
            dma((2, n)),
            dma((2, n)),
            dma((2, groups)),
            dma((2, n, groups)),
            dma((2,)),
        ],
        compiler_params=pltpu.CompilerParams(
            collective_id=0, has_side_effects=True, vmem_limit_bytes=52 * 1024 * 1024
        ),
    )(cholesky, trial_orbitals, blocks, inverse, walkers, drawn, picks)

    potential = potential[:, :rows].reshape(orbitals, orbitals)
    selector = picks[:, 0, :walks].reshape(walk_count, walk_count, n)
    chosen = jnp.einsum("ckb,bkpi->cpi", selector, gathered, preferred_element_type=F32).astype(BF16)
    taylor_term = lax.all_to_all(chosen, "sub", split_axis=0, concat_axis=2, tiled=True)[0]
    summed = taylor_term.astype(F32)
    for degree in range(1, TAYLOR + 1):
        product = jnp.dot(potential, taylor_term, preferred_element_type=F32)
        taylor_term = (product / jnp.float32(degree)).astype(BF16)
        summed = summed + taylor_term.astype(F32)
    propagated = summed.astype(BF16)
    new_walkers = lax.all_to_all(propagated[None], "sub", split_axis=2, concat_axis=0, tiled=True)
    by_walker = bias.reshape(walk_count, n, count)
    force_bias = lax.dynamic_index_in_dim(by_walker, pair_index, 1, False)
    return (new_walkers, force_bias)


def solution(mesh):
    in_specs = (
        P("sub", "pair", None),
        P(),
        P(("grp", "pair", "rep"), None, "sub"),
        P(("grp", "pair", "rep"), None, None),
        P("grp"),
        P("grp"),
        P(("grp", "pair", "rep")),
    )
    out_specs = (P(("grp", "pair", "rep"), None, "sub"), P(("grp", "pair", "rep"), "sub"))
    return jax.shard_map(shards, mesh=mesh, in_specs=in_specs, out_specs=out_specs, check_vma=False)
```

```python
import functools

import jax
import jax.numpy as jnp
from jax import lax
from jax.experimental import pallas as pl
from jax.experimental.pallas import tpu as pltpu
from jax.sharding import PartitionSpec as P

TAYLOR = 6
GROUP = 16
LANES = 128

field_scale = 1.6

MESH = pl.DeviceIdType.MESH
F32 = jnp.float32
BF16 = jnp.bfloat16
NT = (((1,), (1,)), ((), ()))


def step_kernel(
    n, rows, chol, trial, inverse, walkers, drawn, picks, parents,
    walkers_out, bias_out,
    cbuf, wfirst, mixed, mixbuf, wbuf, rbuf, ybuf, ebuf, fbsend, fbbuf, fpad, kron, tmp, keep, psend, precv,
    pfin, pot, xbuf, xsend, done, obuf,
    csem, ssem, msem, xsem, hsem, rsem, fsem, qsem, psem,
):
    a = lax.axis_index("pair")
    s = lax.axis_index("sub")
    groups, count = cbuf.shape[0], cbuf.shape[1]
    electrons, orbitals = trial.shape
    padded = groups * GROUP
    walks = 2 * n
    wide = walks * GROUP
    deep = count * GROUP

    def chol_copy(j):
        return pltpu.make_async_copy(
            chol.at[:, pl.ds(pl.multiple_of(j * GROUP, GROUP), GROUP), :], cbuf.at[j], csem.at[j]
        )

    @pl.loop(0, groups)
    def _(j):
        chol_copy(j).start()

    peers = [(d, lax.rem(a + d, n)) for d in range(1, n)]
    sibling = {"sub": 1 - s}

    def remote(src, dst, sems, place, target):
        return pltpu.make_async_remote_copy(
            src_ref=src, dst_ref=dst, send_sem=sems.at[(0,) + place], recv_sem=sems.at[(1,) + place],
            device_id=target, device_id_type=MESH,
        )

    barrier = pltpu.get_barrier_semaphore()
    pl.semaphore_signal(barrier, inc=1, device_id=sibling, device_id_type=MESH)
    for _, b in peers:
        pl.semaphore_signal(barrier, inc=1, device_id={"pair": b}, device_id_type=MESH)
    pl.semaphore_wait(barrier, n)

    first_copy = remote(walkers.at[1 - s], wfirst.at[s], ssem, (0,), sibling)
    first_copy.start()
    pick_copies = [remote(picks, rbuf.at[:, a], rsem, (d,), {"pair": b}) for d, b in peers]
    for copy in pick_copies:
        copy.start()
    wfirst[s] = walkers[s]
    wbuf[pl.ds(2 * a, 2)] = walkers[...]
    rbuf[:, a] = picks[...]
    if padded != rows:
        spot = lax.broadcasted_iota(jnp.int32, (orbitals, n * padded), 1)
        spot = jnp.where(spot % padded < rows, spot // padded * rows + spot % padded, -1)
        layout = jnp.where(
            spot == lax.broadcasted_iota(jnp.int32, (orbitals, n * padded), 0), 1.0, 0.0
        ).astype(BF16)
    first_copy.wait_recv()
    start = wfirst[...].reshape(electrons, orbitals)
    if padded != rows:
        start = jnp.dot(start, layout, preferred_element_type=F32).astype(BF16)
    mixed[...] = lax.dot_general(
        start, inverse[s], (((0,), (0,)), ((), ())), preferred_element_type=F32
    ).astype(BF16).reshape(n, padded, electrons)

    split = max(1, groups // 2)
    parts = [pl.ds(0, split * GROUP), pl.ds(split * GROUP, (groups - split) * GROUP)]
    mixed_copies = [
        [remote(mixed.at[b, part], mixbuf.at[s, a, part], msem, (h, d), {"pair": b}) for d, b in peers]
        for h, part in enumerate(parts)
    ]
    across_copies = [
        [
            remote(mixbuf.at[s, b, part], mixbuf.at[s, b, part], xsem, (h, d), sibling)
            for d, b in [(d, lax.rem(a + n - d, n)) for d in range(n)]
        ]
        for h, part in enumerate(parts)
    ]
    for h in range(2):
        for copy in mixed_copies[h]:
            copy.start()
    mixbuf[s, a] = mixed[a]

    ybuf[...] = jnp.zeros_like(ybuf)
    fpad[...] = jnp.zeros_like(fpad)
    ebuf[...] = jnp.where(
        lax.broadcasted_iota(jnp.int32, (count, deep), 1) // GROUP
        == lax.broadcasted_iota(jnp.int32, (count, deep), 0), 1.0, 0.0
    ).astype(BF16)

    def chain_copy(way, t):
        block = a - t if way == 0 else a + t
        at = pl.ds(2 * block, 2)
        return remote(wbuf.at[at], wbuf.at[at], hsem, (way, t), {"pair": a + 1 - 2 * way})

    def chain_sends(way, t):
        return (a >= t) & (a + 1 < n) if way == 0 else (a + t < n) & (a > 0)

    def chain_gets(way, t):
        return a >= t + 1 if way == 0 else a + t + 1 < n

    def chain_step(t):
        for way in range(2):
            if t > 0:
                @pl.when(chain_gets(way, t - 1))
                def _():
                    back = a - t if way == 0 else a + t
                    at = pl.ds(2 * back, 2)
                    remote(
                        wbuf.at[at], wbuf.at[at], hsem, (way, t - 1), {"pair": a - 1 + 2 * way}
                    ).wait_recv()
            if t < n - 1:
                @pl.when(chain_sends(way, t))
                def _():
                    chain_copy(way, t).start()

    def pass_across(h):
        across_copies[h][0].start()
        for copy, forward in zip(mixed_copies[h], across_copies[h][1:]):
            copy.wait_recv()
            forward.start()

    tile = max(GROUP, min(deep, 65536 // wide) // GROUP * GROUP)
    share = tile // GROUP

    def bias_group(j):
        chol_copy(j).wait()
        block_rows = mixbuf[:, :, pl.ds(pl.multiple_of(j * GROUP, GROUP), GROUP), :]
        density = jnp.dot(
            block_rows.reshape(wide, electrons), trial[...], preferred_element_type=F32
        ).astype(BF16)

        @pl.loop(0, deep // tile)
        def _(t):
            block = cbuf[j, pl.ds(t * share, share)].reshape(tile, orbitals)
            at = pl.ds(pl.multiple_of(t * tile, tile), tile)
            ybuf[at, :] += lax.dot_general(block, density, NT, preferred_element_type=F32)

    pass_across(0)
    for copy in across_copies[0]:
        copy.wait_recv()
    chain_step(0)
    pl.loop(0, split - 1)(bias_group)
    pass_across(1)
    pl.loop(split - 1, split)(bias_group)
    for copy in across_copies[1]:
        copy.wait_recv()
    late = max(split, groups - 2)
    pl.loop(split, late)(bias_group)
    chain_step(1)
    pl.loop(late, groups)(bias_group)

    same = (
        lax.broadcasted_iota(jnp.int32, (1, GROUP, wide), 1)
        == lax.broadcasted_iota(jnp.int32, (1, GROUP, wide), 2) % GROUP
    )
    traced = jnp.sum(jnp.where(same, ybuf[...].reshape(count, GROUP, wide), 0.0), axis=1)
    adder = jnp.where(
        lax.broadcasted_iota(jnp.int32, (walks, wide), 1) // GROUP
        == lax.broadcasted_iota(jnp.int32, (walks, wide), 0), 1.0, 0.0
    )
    partial = lax.dot_general(
        adder, traced, NT, preferred_element_type=F32, precision=lax.Precision.HIGHEST
    )
    fbsend[...] = partial
    fbbuf[a] = partial
    bias_copies = [remote(fbsend, fbbuf.at[a], fsem, (d,), {"pair": b}) for d, b in peers]
    for copy in bias_copies:
        copy.start()
    for copy in pick_copies + bias_copies:
        copy.wait_recv()
    total = jnp.sum(fbbuf[...], axis=0)
    fpad[0:walks, :] = drawn[...] - total
    fields = fpad[...].astype(BF16)

    step = 8 * GROUP
    chunks = wide // step

    @pl.loop(0, chunks)
    def _(c):
        if chunks == 1:
            chosen = rbuf[...].reshape(step, LANES)
        else:
            per = n // 8
            chosen = rbuf[c // per, pl.ds(lax.rem(c, per) * 8, 8)].reshape(step, LANES)
        spread = jnp.dot(chosen, fields, preferred_element_type=F32).astype(BF16)
        full = jnp.dot(spread, ebuf[...], preferred_element_type=F32)
        diagonal = (
            lax.broadcasted_iota(jnp.int32, (step, deep), 0) % GROUP
            == lax.broadcasted_iota(jnp.int32, (step, deep), 1) % GROUP
        )
        kron[c] = jnp.where(diagonal, full, 0.0).astype(BF16)

    def part_copy(j):
        return remote(psend.at[j], precv.at[j], qsem, (j,), sibling)

    def pot_copy(d, b, j):
        at = pl.ds(pl.multiple_of(j * GROUP, GROUP), GROUP)
        return remote(pfin.at[b, at], pot.at[a, at], psem, (d, j), {"pair": b})

    def finish(j):
        part_copy(j).wait_recv()
        at = pl.ds(pl.multiple_of(j * GROUP, GROUP), GROUP)
        pfin[:, at, :] = (field_scale * (keep[j] + precv[j].astype(F32))).astype(BF16)
        for d, b in peers:
            pot_copy(d, b, j).start()

    def potential_group(j):
        @pl.loop(0, chunks)
        def _(c):
            tmp[pl.ds(c * 8, 8)] = jnp.dot(
                kron[c], cbuf[j].reshape(deep, orbitals), preferred_element_type=F32
            ).reshape(8, GROUP, orbitals)

        psend[j] = tmp[pl.ds((1 - s) * n, n)].astype(BF16)
        part_copy(j).start()
        keep[j] = tmp[pl.ds(s * n, n)]

        @pl.when(j > 0)
        def _():
            finish(j - 1)

    early = min(3, groups)
    pl.loop(0, early)(potential_group)
    if n > 2:
        chain_step(2)
    pl.loop(early, groups)(potential_group)
    finish(groups - 1)
    pot[a] = pfin[a]

    fbsend_rows = fpad.at[0:walks]
    fbsend_rows[...] = total
    for k in range(2):
        bias_out[k : k + 1, :] = fpad[pl.ds(k * n + a, 1), :]

    for t in range(3, n):
        chain_step(t)
    xbuf[s] = wbuf[parents[s]]
    xsend[...] = wbuf[parents[1 - s]]
    child_copy = remote(xsend, xbuf.at[s], ssem, (1,), sibling)
    child_copy.start()
    child_copy.wait_recv()
    term = xbuf[...].reshape(electrons, orbitals)
    summed = term.astype(F32)

    @pl.loop(0, groups)
    def _(j):
        for d, b in peers:
            pot_copy(d, b, j).wait_recv()

    for degree in range(1, TAYLOR + 1):
        product = lax.dot_general(
            term, pot[...].reshape(n * padded, orbitals), NT, preferred_element_type=F32
        )
        term = (product / jnp.float32(degree)).astype(BF16)
        if padded != rows:
            term = lax.dot_general(term, layout, NT, preferred_element_type=F32).astype(BF16)
        summed = summed + term.astype(F32)
    done[...] = summed.astype(BF16).reshape(done.shape)
    last_copy = remote(done.at[1 - s], obuf.at[s], ssem, (2,), sibling)
    last_copy.start()
    obuf[s] = done[s]

    first_copy.wait_send()
    child_copy.wait_send()
    for copy in mixed_copies[0] + mixed_copies[1] + across_copies[0] + across_copies[1]:
        copy.wait_send()
    for copy in pick_copies + bias_copies:
        copy.wait_send()
    for t in range(n - 1):
        for way in range(2):
            @pl.when(chain_sends(way, t))
            def _():
                chain_copy(way, t).wait_send()

    @pl.loop(0, groups)
    def _(j):
        part_copy(j).wait_send()
        for d, b in peers:
            pot_copy(d, b, j).wait_send()

    last_copy.wait()
    walkers_out[...] = obuf[...]


def shards(cholesky, trial_orbitals, walkers, intersection_inverse, noise_stream, offsets, parents):
    count, rows, orbitals = cholesky.shape
    walk_count, _, half = walkers.shape
    electrons = trial_orbitals.shape[1]
    n = lax.axis_size("pair")
    rep_size = lax.axis_size("rep")
    rep_index = lax.axis_index("rep")
    sub_index = lax.axis_index("sub")
    assert walk_count == 2 and lax.axis_size("sub") == 2
    padded = -(-rows // GROUP) * GROUP
    groups = padded // GROUP
    walks = walk_count * n
    wide, deep = walks * GROUP, count * GROUP
    split = max(1, groups // 2)
    if padded != rows:
        cholesky = jnp.pad(cholesky, ((0, 0), (0, padded - rows), (0, 0)))

    offsets_grid = offsets.reshape(n, rep_size, walk_count)
    row_offsets = lax.dynamic_index_in_dim(offsets_grid, rep_index, 1, False).T.reshape(-1)
    wanted = row_offsets[:, None] + sub_index * count + jnp.arange(count, dtype=jnp.int32)[None, :]
    places = jnp.arange(noise_stream.shape[0], dtype=jnp.int32)
    drawn = jnp.sum(
        jnp.where(wanted[:, :, None] == places[None, None, :], noise_stream[None, None, :], 0.0), axis=2
    )

    columns = (parents % walk_count) * n + parents // walk_count
    picks = (columns[:, None] == jnp.arange(LANES, dtype=jnp.int32)[None, :]).astype(BF16)
    picks = jnp.broadcast_to(picks[:, None, :], (walk_count, GROUP, LANES))

    vmem = pl.BlockSpec(memory_space=pltpu.VMEM)
    smem = pl.BlockSpec(memory_space=pltpu.SMEM)
    hbm = pl.BlockSpec(memory_space=pl.ANY)
    dma = pltpu.SemaphoreType.DMA
    new_walkers, force_bias = pl.pallas_call(
        functools.partial(step_kernel, n, rows),
        out_shape=(
            jax.ShapeDtypeStruct((walk_count, half, orbitals), BF16),
            jax.ShapeDtypeStruct((walk_count, count), F32),
        ),
        in_specs=[hbm, vmem, vmem, vmem, vmem, vmem, smem],
        out_specs=(vmem, vmem),
        scratch_shapes=[
            pltpu.VMEM((groups, count, GROUP, orbitals), BF16),
            pltpu.VMEM((2, half, orbitals), BF16),
            pltpu.VMEM((n, padded, electrons), BF16),
            pltpu.VMEM((2, n, padded, electrons), BF16),
            pltpu.VMEM((walks, half, orbitals), BF16),
            pltpu.VMEM((2, n, GROUP, LANES), BF16),
            pltpu.VMEM((deep, wide), F32),
            pltpu.VMEM((count, deep), BF16),
            pltpu.VMEM((walks, count), F32),
            pltpu.VMEM((n, walks, count), F32),
            pltpu.VMEM((LANES, count), F32),
            pltpu.VMEM((wide // (8 * GROUP), 8 * GROUP, deep), BF16),
            pltpu.VMEM((walks, GROUP, orbitals), F32),
            pltpu.VMEM((groups, n, GROUP, orbitals), F32),
            pltpu.VMEM((groups, n, GROUP, orbitals), BF16),
            pltpu.VMEM((groups, n, GROUP, orbitals), BF16),
            pltpu.VMEM((n, padded, orbitals), BF16),
            pltpu.VMEM((n, padded, orbitals), BF16),
            pltpu.VMEM((2, half, orbitals), BF16),
            pltpu.VMEM((half, orbitals), BF16),
            pltpu.VMEM((2, half, orbitals), BF16),
            pltpu.VMEM((2, half, orbitals), BF16),
            dma((groups,)),
            dma((2, 3)),
            dma((2, 2, n)),
            dma((2, 2, n)),
            dma((2, 2, n)),
            dma((2, n)),
            dma((2, n)),
            dma((2, groups)),
            dma((2, n, groups)),
        ],
        compiler_params=pltpu.CompilerParams(
            collective_id=0, has_side_effects=True, vmem_limit_bytes=56 * 1024 * 1024
        ),
    )(
        cholesky, trial_orbitals.T, intersection_inverse, jnp.swapaxes(walkers, 1, 2), drawn, picks, parents
    )
    return (jnp.swapaxes(new_walkers, 1, 2), force_bias)


def solution(mesh):
    in_specs = (
        P("sub", "pair", None),
        P(),
        P(("grp", "pair", "rep"), None, "sub"),
        P(("grp", "pair", "rep"), None, None),
        P("grp"),
        P("grp"),
        P(("grp", "pair", "rep")),
    )
    out_specs = (P(("grp", "pair", "rep"), None, "sub"), P(("grp", "pair", "rep"), "sub"))
    return jax.shard_map(shards, mesh=mesh, in_specs=in_specs, out_specs=out_specs, check_vma=False)
```

```python
import functools

import jax
import jax.numpy as jnp
from jax import lax
from jax.experimental import pallas as pl
from jax.experimental.pallas import tpu as pltpu
from jax.sharding import PartitionSpec as P

TAYLOR = 6
GROUP = 16
LANES = 128

field_scale = 1.6

MESH = pl.DeviceIdType.MESH
F32 = jnp.float32
BF16 = jnp.bfloat16
NT = (((1,), (1,)), ((), ()))


def step_kernel(
    n, rows, chol, trial, inverse, walkers, noise, offsets, parents,
    walkers_out, bias_out,
    cbuf, wfirst, mixed, mixbuf, wbuf, rbuf, ybuf, ebuf, fbsend, fbbuf, fpad, kron, tmp, keep, psend, precv,
    pfin, pot, xbuf, xsend, done, obuf, picks, window,
    csem, ssem, msem, xsem, hsem, rsem, fsem, qsem, psem,
):
    a = lax.axis_index("pair")
    s = lax.axis_index("sub")
    groups, count = cbuf.shape[0], cbuf.shape[1]
    electrons, orbitals = trial.shape
    padded = groups * GROUP
    walks = 2 * n
    wide = walks * GROUP
    deep = count * GROUP

    def chol_copy(j):
        return pltpu.make_async_copy(
            chol.at[:, pl.ds(pl.multiple_of(j * GROUP, GROUP), GROUP), :], cbuf.at[j], csem.at[j]
        )

    @pl.loop(0, groups)
    def _(j):
        chol_copy(j).start()

    peers = [(d, lax.rem(a + d, n)) for d in range(1, n)]
    sibling = {"sub": 1 - s}

    def remote(src, dst, sems, place, target):
        return pltpu.make_async_remote_copy(
            src_ref=src, dst_ref=dst, send_sem=sems.at[(0,) + place], recv_sem=sems.at[(1,) + place],
            device_id=target, device_id_type=MESH,
        )

    spots = lax.broadcasted_iota(jnp.int32, (GROUP, LANES), 1)
    for k in range(2):
        column = lax.rem(parents[k], 2) * n + lax.div(parents[k], 2)
        picks[k] = jnp.where(spots == column, 1.0, 0.0).astype(BF16)

    barrier = pltpu.get_barrier_semaphore()
    pl.semaphore_signal(barrier, inc=1, device_id=sibling, device_id_type=MESH)
    for _, b in peers:
        pl.semaphore_signal(barrier, inc=1, device_id={"pair": b}, device_id_type=MESH)
    pl.semaphore_wait(barrier, n)

    first_copy = remote(walkers.at[1 - s], wfirst.at[s], ssem, (0,), sibling)
    first_copy.start()
    pick_copies = [remote(picks, rbuf.at[:, a], rsem, (d,), {"pair": b}) for d, b in peers]
    for copy in pick_copies:
        copy.start()
    wfirst[s] = walkers[s]
    wbuf[pl.ds(2 * a, 2)] = walkers[...]
    rbuf[:, a] = picks[...]
    if padded != rows:
        spot = lax.broadcasted_iota(jnp.int32, (orbitals, n * padded), 1)
        spot = jnp.where(spot % padded < rows, spot // padded * rows + spot % padded, -1)
        layout = jnp.where(
            spot == lax.broadcasted_iota(jnp.int32, (orbitals, n * padded), 0), 1.0, 0.0
        ).astype(BF16)
    first_copy.wait_recv()
    start = wfirst[...].reshape(electrons, orbitals)
    if padded != rows:
        start = jnp.dot(start, layout, preferred_element_type=F32).astype(BF16)
    mixed[...] = lax.dot_general(
        start, inverse[s], (((0,), (0,)), ((), ())), preferred_element_type=F32
    ).astype(BF16).reshape(n, padded, electrons)

    split = max(1, groups // 2)
    parts = [pl.ds(0, split * GROUP), pl.ds(split * GROUP, (groups - split) * GROUP)]
    mixed_copies = [
        [remote(mixed.at[b, part], mixbuf.at[s, a, part], msem, (h, d), {"pair": b}) for d, b in peers]
        for h, part in enumerate(parts)
    ]
    across_copies = [
        [
            remote(mixbuf.at[s, b, part], mixbuf.at[s, b, part], xsem, (h, d), sibling)
            for d, b in [(d, lax.rem(a + n - d, n)) for d in range(n)]
        ]
        for h, part in enumerate(parts)
    ]
    for h in range(2):
        for copy in mixed_copies[h]:
            copy.start()
    mixbuf[s, a] = mixed[a]

    rep, rep_size = lax.axis_index("rep"), lax.axis_size("rep")
    low = jnp.zeros((walks, 2 * LANES), jnp.int32)
    number = lax.broadcasted_iota(jnp.int32, (walks, 2 * LANES), 0)
    for b in range(n):
        for k in range(2):
            place = offsets[(b * rep_size + rep) * 2 + k] + s * count
            row = lax.div(place, LANES)
            w = k * n + b
            window[w : w + 1, 0:LANES] = noise[pl.ds(row, 1), :]
            after = jnp.minimum(row + 1, noise.shape[0] - 1)
            window[w : w + 1, LANES:] = noise[pl.ds(after, 1), :]
            low = jnp.where(number == w, lax.rem(place, LANES), low)
    seen = window[...]
    amount = 1
    while amount < LANES:
        turned = jnp.concatenate([seen[:, amount:], seen[:, :amount]], axis=1)
        seen = jnp.where(lax.rem(lax.div(low, amount), 2) == 1, turned, seen)
        amount *= 2
    window[...] = seen

    ybuf[...] = jnp.zeros_like(ybuf)
    fpad[...] = jnp.zeros_like(fpad)
    ebuf[...] = jnp.where(
        lax.broadcasted_iota(jnp.int32, (count, deep), 1) // GROUP
        == lax.broadcasted_iota(jnp.int32, (count, deep), 0), 1.0, 0.0
    ).astype(BF16)

    def chain_copy(way, t):
        block = a - t if way == 0 else a + t
        at = pl.ds(2 * block, 2)
        return remote(wbuf.at[at], wbuf.at[at], hsem, (way, t), {"pair": a + 1 - 2 * way})

    def chain_sends(way, t):
        return (a >= t) & (a + 1 < n) if way == 0 else (a + t < n) & (a > 0)

    def chain_gets(way, t):
        return a >= t + 1 if way == 0 else a + t + 1 < n

    def chain_step(t):
        for way in range(2):
            if t > 0:
                @pl.when(chain_gets(way, t - 1))
                def _():
                    back = a - t if way == 0 else a + t
                    at = pl.ds(2 * back, 2)
                    remote(
                        wbuf.at[at], wbuf.at[at], hsem, (way, t - 1), {"pair": a - 1 + 2 * way}
                    ).wait_recv()
            if t < n - 1:
                @pl.when(chain_sends(way, t))
                def _():
                    chain_copy(way, t).start()

    def pass_across(h):
        across_copies[h][0].start()
        for copy, forward in zip(mixed_copies[h], across_copies[h][1:]):
            copy.wait_recv()
            forward.start()

    tile = max(GROUP, min(deep, 131072 // wide) // GROUP * GROUP)
    share = tile // GROUP

    def bias_group(j):
        chol_copy(j).wait()
        block_rows = mixbuf[:, :, pl.ds(pl.multiple_of(j * GROUP, GROUP), GROUP), :]
        density = jnp.dot(
            block_rows.reshape(wide, electrons), trial[...], preferred_element_type=F32
        ).astype(BF16)

        @pl.loop(0, deep // tile)
        def _(t):
            block = cbuf[j, pl.ds(t * share, share)].reshape(tile, orbitals)
            at = pl.ds(pl.multiple_of(t * tile, tile), tile)
            ybuf[at, :] += lax.dot_general(block, density, NT, preferred_element_type=F32)

    pass_across(0)
    for copy in across_copies[0]:
        copy.wait_recv()
    chain_step(0)
    pl.loop(0, split - 1)(bias_group)
    pass_across(1)
    pl.loop(split - 1, split)(bias_group)
    for copy in across_copies[1]:
        copy.wait_recv()
    late = max(split, groups - 2)
    pl.loop(split, late)(bias_group)
    chain_step(1)
    pl.loop(late, groups)(bias_group)

    same = (
        lax.broadcasted_iota(jnp.int32, (1, GROUP, wide), 1)
        == lax.broadcasted_iota(jnp.int32, (1, GROUP, wide), 2) % GROUP
    )
    traced = jnp.sum(jnp.where(same, ybuf[...].reshape(count, GROUP, wide), 0.0), axis=1)
    adder = jnp.where(
        lax.broadcasted_iota(jnp.int32, (walks, wide), 1) // GROUP
        == lax.broadcasted_iota(jnp.int32, (walks, wide), 0), 1.0, 0.0
    )
    partial = lax.dot_general(
        adder, traced, NT, preferred_element_type=F32, precision=lax.Precision.HIGHEST
    )
    fbsend[...] = partial
    fbbuf[a] = partial
    bias_copies = [remote(fbsend, fbbuf.at[a], fsem, (d,), {"pair": b}) for d, b in peers]
    for copy in bias_copies:
        copy.start()
    for copy in pick_copies + bias_copies:
        copy.wait_recv()
    total = jnp.sum(fbbuf[...], axis=0)
    fpad[0:walks, :] = window[:, 0:LANES] - total
    fields = fpad[...].astype(BF16)

    step = 8 * GROUP
    chunks = wide // step

    @pl.loop(0, chunks)
    def _(c):
        if chunks == 1:
            chosen = rbuf[...].reshape(step, LANES)
        else:
            per = n // 8
            chosen = rbuf[c // per, pl.ds(lax.rem(c, per) * 8, 8)].reshape(step, LANES)
        spread = jnp.dot(chosen, fields, preferred_element_type=F32).astype(BF16)
        full = jnp.dot(spread, ebuf[...], preferred_element_type=F32)
        diagonal = (
            lax.broadcasted_iota(jnp.int32, (step, deep), 0) % GROUP
            == lax.broadcasted_iota(jnp.int32, (step, deep), 1) % GROUP
        )
        kron[c] = jnp.where(diagonal, full, 0.0).astype(BF16)

    def part_copy(j):
        return remote(psend.at[j], precv.at[j], qsem, (j,), sibling)

    def pot_copy(d, b, j):
        at = pl.ds(pl.multiple_of(j * GROUP, GROUP), GROUP)
        return remote(pfin.at[b, at], pot.at[a, at], psem, (d, j), {"pair": b})

    def finish(j):
        part_copy(j).wait_recv()
        at = pl.ds(pl.multiple_of(j * GROUP, GROUP), GROUP)
        pfin[:, at, :] = (field_scale * (keep[j] + precv[j].astype(F32))).astype(BF16)
        for d, b in peers:
            pot_copy(d, b, j).start()

    def potential_group(j):
        @pl.loop(0, chunks)
        def _(c):
            tmp[pl.ds(c * 8, 8)] = jnp.dot(
                kron[c], cbuf[j].reshape(deep, orbitals), preferred_element_type=F32
            ).reshape(8, GROUP, orbitals)

        psend[j] = tmp[pl.ds((1 - s) * n, n)].astype(BF16)
        part_copy(j).start()
        keep[j] = tmp[pl.ds(s * n, n)]

        @pl.when(j > 0)
        def _():
            finish(j - 1)

    early = min(3, groups)
    pl.loop(0, early)(potential_group)
    if n > 2:
        chain_step(2)
    pl.loop(early, groups)(potential_group)
    finish(groups - 1)
    pot[a] = pfin[a]

    fbsend_rows = fpad.at[0:walks]
    fbsend_rows[...] = total
    for k in range(2):
        bias_out[k : k + 1, :] = fpad[pl.ds(k * n + a, 1), :]

    for t in range(3, n):
        chain_step(t)
    xbuf[s] = wbuf[parents[s]]
    xsend[...] = wbuf[parents[1 - s]]
    child_copy = remote(xsend, xbuf.at[s], ssem, (1,), sibling)
    child_copy.start()
    child_copy.wait_recv()
    eye = jnp.where(
        lax.broadcasted_iota(jnp.int32, (electrons, electrons), 0)
        == lax.broadcasted_iota(jnp.int32, (electrons, electrons), 1), 1.0, 0.0
    ).astype(BF16)
    term = lax.dot_general(
        xbuf[...].reshape(electrons, orbitals), eye, (((0,), (0,)), ((), ())), preferred_element_type=F32
    ).astype(BF16)
    summed = term.astype(F32)

    @pl.loop(0, groups)
    def _(j):
        for d, b in peers:
            pot_copy(d, b, j).wait_recv()

    for degree in range(1, TAYLOR + 1):
        product = jnp.dot(
            pot[...].reshape(n * padded, orbitals), term, preferred_element_type=F32
        )
        term = (product / jnp.float32(degree)).astype(BF16)
        if padded != rows:
            term = jnp.dot(layout, term, preferred_element_type=F32).astype(BF16)
        summed = summed + term.astype(F32)
    done[...] = lax.dot_general(
        eye, summed.astype(BF16), NT, preferred_element_type=F32
    ).astype(BF16).reshape(done.shape)
    last_copy = remote(done.at[1 - s], obuf.at[s], ssem, (2,), sibling)
    last_copy.start()
    obuf[s] = done[s]

    first_copy.wait_send()
    child_copy.wait_send()
    for copy in mixed_copies[0] + mixed_copies[1] + across_copies[0] + across_copies[1]:
        copy.wait_send()
    for copy in pick_copies + bias_copies:
        copy.wait_send()
    for t in range(n - 1):
        for way in range(2):
            @pl.when(chain_sends(way, t))
            def _():
                chain_copy(way, t).wait_send()

    @pl.loop(0, groups)
    def _(j):
        part_copy(j).wait_send()
        for d, b in peers:
            pot_copy(d, b, j).wait_send()

    last_copy.wait()
    walkers_out[...] = obuf[...]


def shards(cholesky, trial_orbitals, walkers, intersection_inverse, noise_stream, offsets, parents):
    count, rows, orbitals = cholesky.shape
    walk_count, _, half = walkers.shape
    electrons = trial_orbitals.shape[1]
    n = lax.axis_size("pair")
    assert walk_count == 2 and lax.axis_size("sub") == 2 and count == LANES
    padded = -(-rows // GROUP) * GROUP
    groups = padded // GROUP
    walks = walk_count * n
    wide, deep = walks * GROUP, count * GROUP
    if padded != rows:
        cholesky = jnp.pad(cholesky, ((0, 0), (0, padded - rows), (0, 0)))

    vmem = pl.BlockSpec(memory_space=pltpu.VMEM)
    smem = pl.BlockSpec(memory_space=pltpu.SMEM)
    hbm = pl.BlockSpec(memory_space=pl.ANY)
    dma = pltpu.SemaphoreType.DMA
    new_walkers, force_bias = pl.pallas_call(
        functools.partial(step_kernel, n, rows),
        out_shape=(
            jax.ShapeDtypeStruct((walk_count, half, orbitals), BF16),
            jax.ShapeDtypeStruct((walk_count, count), F32),
        ),
        in_specs=[hbm, vmem, vmem, vmem, vmem, smem, smem],
        out_specs=(vmem, vmem),
        scratch_shapes=[
            pltpu.VMEM((groups, count, GROUP, orbitals), BF16),
            pltpu.VMEM((2, half, orbitals), BF16),
            pltpu.VMEM((n, padded, electrons), BF16),
            pltpu.VMEM((2, n, padded, electrons), BF16),
            pltpu.VMEM((walks, half, orbitals), BF16),
            pltpu.VMEM((2, n, GROUP, LANES), BF16),
            pltpu.VMEM((deep, wide), F32),
            pltpu.VMEM((count, deep), BF16),
            pltpu.VMEM((walks, count), F32),
            pltpu.VMEM((n, walks, count), F32),
            pltpu.VMEM((LANES, count), F32),
            pltpu.VMEM((wide // (8 * GROUP), 8 * GROUP, deep), BF16),
            pltpu.VMEM((walks, GROUP, orbitals), F32),
            pltpu.VMEM((groups, n, GROUP, orbitals), F32),
            pltpu.VMEM((groups, n, GROUP, orbitals), BF16),
            pltpu.VMEM((groups, n, GROUP, orbitals), BF16),
            pltpu.VMEM((n, padded, orbitals), BF16),
            pltpu.VMEM((n, padded, orbitals), BF16),
            pltpu.VMEM((2, half, orbitals), BF16),
            pltpu.VMEM((half, orbitals), BF16),
            pltpu.VMEM((2, half, orbitals), BF16),
            pltpu.VMEM((2, half, orbitals), BF16),
            pltpu.VMEM((walk_count, GROUP, LANES), BF16),
            pltpu.VMEM((walks, 2 * LANES), F32),
            dma((groups,)),
            dma((2, 3)),
            dma((2, 2, n)),
            dma((2, 2, n)),
            dma((2, 2, n)),
            dma((2, n)),
            dma((2, n)),
            dma((2, groups)),
            dma((2, n, groups)),
        ],
        compiler_params=pltpu.CompilerParams(
            collective_id=0, has_side_effects=True, vmem_limit_bytes=44 * 1024 * 1024
        ),
    )(
        cholesky, trial_orbitals.T, intersection_inverse, jnp.swapaxes(walkers, 1, 2),
        noise_stream.reshape(-1, LANES), offsets, parents,
    )
    return (jnp.swapaxes(new_walkers, 1, 2), force_bias)


def solution(mesh):
    in_specs = (
        P("sub", "pair", None),
        P(),
        P(("grp", "pair", "rep"), None, "sub"),
        P(("grp", "pair", "rep"), None, None),
        P("grp"),
        P("grp"),
        P(("grp", "pair", "rep")),
    )
    out_specs = (P(("grp", "pair", "rep"), None, "sub"), P(("grp", "pair", "rep"), "sub"))
    return jax.shard_map(shards, mesh=mesh, in_specs=in_specs, out_specs=out_specs, check_vma=False)
```

```python
import functools

import jax
import jax.numpy as jnp
from jax import lax
from jax.experimental import pallas as pl
from jax.experimental.pallas import tpu as pltpu
from jax.sharding import PartitionSpec as P

TAYLOR = 6
GROUP = 16
LANES = 128

field_scale = 1.6

MESH = pl.DeviceIdType.MESH
F32 = jnp.float32
BF16 = jnp.bfloat16
NT = (((1,), (1,)), ((), ()))


def step_kernel(
    n, ways, rows, chol, trial_in, inverse_in, walkers_in, noise_in, offsets, parents,
    walkers_out, bias_out,
    cbuf, wfirst, mixed, mixbuf, wbuf, rbuf, ybuf, ebuf, fbsend, fbbuf, fpad, kron, tmp, keep, psend, precv,
    pfin, pot, xbuf, xsend, done, obuf, picks, window, trial, inverse, noise,
    csem, ssem, msem, xsem, hsem, rsem, fsem, qsem, psem, isem,
):
    a = lax.axis_index("pair")
    s = lax.axis_index("sub")
    groups, count = cbuf.shape[0], cbuf.shape[1]
    electrons, orbitals = trial.shape
    every = n * ways
    q = lax.axis_index("rep") if ways > 1 else 0
    me = q * n + a
    span = groups * GROUP
    padded = span * ways
    walks = 2 * every
    wide = walks * GROUP
    deep = count * GROUP

    def chol_copy(j):
        return pltpu.make_async_copy(
            chol.at[:, pl.ds(pl.multiple_of(q * span + j * GROUP, GROUP), GROUP), :],
            cbuf.at[j], csem.at[j],
        )

    own_walkers = pl.ds(2 * a, 2)
    loads = [
        pltpu.make_async_copy(src, dst, isem.at[i])
        for i, (src, dst) in enumerate(
            [(walkers_in, wbuf.at[own_walkers]), (inverse_in, inverse), (noise_in, noise), (trial_in, trial)]
        )
    ]
    for load in loads:
        load.start()

    @pl.loop(0, groups)
    def _(j):
        chol_copy(j).start()

    peers = [(d, lax.rem(me + d, every)) for d in range(1, every)]

    def holder(c):
        return {"pair": lax.rem(c, n), "rep": lax.div(c, n)} if ways > 1 else {"pair": c}
    sibling = {"sub": 1 - s}

    def remote(src, dst, sems, place, target):
        return pltpu.make_async_remote_copy(
            src_ref=src, dst_ref=dst, send_sem=sems.at[(0,) + place], recv_sem=sems.at[(1,) + place],
            device_id=target, device_id_type=MESH,
        )

    spots = lax.broadcasted_iota(jnp.int32, (GROUP, LANES), 1)
    for k in range(2):
        column = lax.rem(parents[k], 2) * every + q * n + lax.div(parents[k], 2)
        picks[k] = jnp.where(spots == column, 1.0, 0.0).astype(BF16)

    barrier = pltpu.get_barrier_semaphore()
    pl.semaphore_signal(barrier, inc=1, device_id=sibling, device_id_type=MESH)
    for _, c in peers:
        pl.semaphore_signal(barrier, inc=1, device_id=holder(c), device_id_type=MESH)
    loads[0].wait()
    pl.semaphore_wait(barrier, every)

    first_copy = remote(wbuf.at[2 * a + 1 - s], wfirst.at[s], ssem, (0,), sibling)
    first_copy.start()
    pick_copies = [remote(picks, rbuf.at[:, me], rsem, (d,), holder(c)) for d, c in peers]
    for copy in pick_copies:
        copy.start()
    wfirst[s] = wbuf[2 * a + s]
    rbuf[:, me] = picks[...]
    loads[1].wait()
    loads[2].wait()
    if padded != rows:
        spot = lax.broadcasted_iota(jnp.int32, (orbitals, n * padded), 1)
        spot = jnp.where(spot % padded < rows, spot // padded * rows + spot % padded, -1)
        layout = jnp.where(
            spot == lax.broadcasted_iota(jnp.int32, (orbitals, n * padded), 0), 1.0, 0.0
        ).astype(BF16)
    first_copy.wait_recv()
    start = wfirst[...].reshape(electrons, orbitals)
    if padded != rows:
        start = jnp.dot(start, layout, preferred_element_type=F32).astype(BF16)
    mixed[...] = lax.dot_general(
        start, inverse[s], (((0,), (0,)), ((), ())), preferred_element_type=F32
    ).astype(BF16).reshape(n, ways, span, electrons)

    split = max(1, groups // 2)
    parts = [pl.ds(0, split * GROUP), pl.ds(split * GROUP, (groups - split) * GROUP)]
    mixed_copies = [
        [
            remote(
                mixed.at[lax.rem(c, n), lax.div(c, n), part], mixbuf.at[s, me, part], msem, (h, d), holder(c)
            )
            for d, c in peers
        ]
        for h, part in enumerate(parts)
    ]
    across_copies = [
        [
            remote(mixbuf.at[s, c, part], mixbuf.at[s, c, part], xsem, (h, d), sibling)
            for d, c in [(d, lax.rem(me + every - d, every)) for d in range(every)]
        ]
        for h, part in enumerate(parts)
    ]
    for h in range(2):
        for copy in mixed_copies[h]:
            copy.start()
    mixbuf[s, me] = mixed[a, q]

    rep, rep_size = lax.axis_index("rep"), lax.axis_size("rep")
    low = jnp.zeros((walks, 2 * LANES), jnp.int32)
    number = lax.broadcasted_iota(jnp.int32, (walks, 2 * LANES), 0)
    for c in range(every):
        for k in range(2):
            home = c // n if ways > 1 else rep
            place = offsets[(c % n * rep_size + home) * 2 + k] + s * count
            row = lax.div(place, LANES)
            w = k * every + c
            window[w : w + 1, 0:LANES] = noise[pl.ds(row, 1), :]
            after = jnp.minimum(row + 1, noise.shape[0] - 1)
            window[w : w + 1, LANES:] = noise[pl.ds(after, 1), :]
            low = jnp.where(number == w, lax.rem(place, LANES), low)
    seen = window[...]
    amount = 1
    while amount < LANES:
        turned = jnp.concatenate([seen[:, amount:], seen[:, :amount]], axis=1)
        seen = jnp.where(lax.rem(lax.div(low, amount), 2) == 1, turned, seen)
        amount *= 2
    window[...] = seen

    ybuf[...] = jnp.zeros_like(ybuf)
    fpad[...] = jnp.zeros_like(fpad)
    ebuf[...] = jnp.where(
        lax.broadcasted_iota(jnp.int32, (count, deep), 1) // GROUP
        == lax.broadcasted_iota(jnp.int32, (count, deep), 0), 1.0, 0.0
    ).astype(BF16)

    def chain_copy(way, t):
        block = a - t if way == 0 else a + t
        at = pl.ds(2 * block, 2)
        return remote(wbuf.at[at], wbuf.at[at], hsem, (way, t), {"pair": a + 1 - 2 * way})

    def chain_sends(way, t):
        return (a >= t) & (a + 1 < n) if way == 0 else (a + t < n) & (a > 0)

    def chain_gets(way, t):
        return a >= t + 1 if way == 0 else a + t + 1 < n

    def chain_step(t):
        for way in range(2):
            if t > 0:
                @pl.when(chain_gets(way, t - 1))
                def _():
                    back = a - t if way == 0 else a + t
                    at = pl.ds(2 * back, 2)
                    remote(
                        wbuf.at[at], wbuf.at[at], hsem, (way, t - 1), {"pair": a - 1 + 2 * way}
                    ).wait_recv()
            if t < n - 1:
                @pl.when(chain_sends(way, t))
                def _():
                    chain_copy(way, t).start()

    def pass_across(h):
        across_copies[h][0].start()
        for copy, forward in zip(mixed_copies[h], across_copies[h][1:]):
            copy.wait_recv()
            forward.start()

    tile = max(GROUP, min(deep, 262144 // wide) // GROUP * GROUP)
    share = tile // GROUP

    def bias_group(j):
        chol_copy(j).wait()
        block_rows = mixbuf[:, :, pl.ds(pl.multiple_of(j * GROUP, GROUP), GROUP), :]
        density = jnp.dot(
            block_rows.reshape(wide, electrons), trial[...], preferred_element_type=F32
        ).astype(BF16)

        @pl.loop(0, deep // tile)
        def _(t):
            block = cbuf[j, pl.ds(t * share, share)].reshape(tile, orbitals)
            at = pl.ds(pl.multiple_of(t * tile, tile), tile)
            ybuf[at, :] += lax.dot_general(block, density, NT, preferred_element_type=F32)

    pass_across(0)
    for copy in across_copies[0]:
        copy.wait_recv()
    chain_step(0)
    loads[3].wait()
    pl.loop(0, split - 1)(bias_group)
    pass_across(1)
    pl.loop(split - 1, split)(bias_group)
    for copy in across_copies[1]:
        copy.wait_recv()
    late = max(split, groups - 2)
    pl.loop(split, late)(bias_group)
    chain_step(1)
    pl.loop(late, groups)(bias_group)

    same = (
        lax.broadcasted_iota(jnp.int32, (1, GROUP, wide), 1)
        == lax.broadcasted_iota(jnp.int32, (1, GROUP, wide), 2) % GROUP
    )
    traced = jnp.sum(jnp.where(same, ybuf[...].reshape(count, GROUP, wide), 0.0), axis=1)
    adder = jnp.where(
        lax.broadcasted_iota(jnp.int32, (walks, wide), 1) // GROUP
        == lax.broadcasted_iota(jnp.int32, (walks, wide), 0), 1.0, 0.0
    )
    partial = lax.dot_general(
        adder, traced, NT, preferred_element_type=F32, precision=lax.Precision.HIGHEST
    )
    fbsend[...] = partial
    fbbuf[me] = partial
    bias_copies = [remote(fbsend, fbbuf.at[me], fsem, (d,), holder(c)) for d, c in peers]
    for copy in bias_copies:
        copy.start()
    for copy in pick_copies + bias_copies:
        copy.wait_recv()
    total = jnp.sum(fbbuf[...], axis=0)
    fpad[0:walks, :] = window[:, 0:LANES] - total
    fields = fpad[...].astype(BF16)

    some = min(16, walks)
    step = some * GROUP
    chunks = wide // step

    @pl.loop(0, chunks)
    def _(c):
        if chunks == 1:
            chosen = rbuf[...].reshape(step, LANES)
        else:
            per = every // some
            chosen = rbuf[c // per, pl.ds(lax.rem(c, per) * some, some)].reshape(step, LANES)
        spread = jnp.dot(chosen, fields, preferred_element_type=F32).astype(BF16)
        full = jnp.dot(spread, ebuf[...], preferred_element_type=F32)
        diagonal = (
            lax.broadcasted_iota(jnp.int32, (step, deep), 0) % GROUP
            == lax.broadcasted_iota(jnp.int32, (step, deep), 1) % GROUP
        )
        kron[c] = jnp.where(diagonal, full, 0.0).astype(BF16)

    def part_copy(j):
        return remote(psend.at[j], precv.at[j], qsem, (j,), sibling)

    def pot_copy(d, c, j):
        at = pl.ds(pl.multiple_of(j * GROUP, GROUP), GROUP)
        return remote(pfin.at[c, at], pot.at[a, q, at], psem, (d, j), holder(c))

    def finish(j):
        part_copy(j).wait_recv()
        at = pl.ds(pl.multiple_of(j * GROUP, GROUP), GROUP)
        pfin[:, at, :] = (field_scale * (keep[j] + precv[j].astype(F32))).astype(BF16)
        for d, b in peers:
            pot_copy(d, b, j).start()

    def potential_group(j):
        @pl.loop(0, chunks)
        def _(c):
            tmp[pl.ds(c * some, some)] = jnp.dot(
                kron[c], cbuf[j].reshape(deep, orbitals), preferred_element_type=F32
            ).reshape(some, GROUP, orbitals)

        psend[j] = tmp[pl.ds((1 - s) * every, every)].astype(BF16)
        part_copy(j).start()
        keep[j] = tmp[pl.ds(s * every, every)]

        @pl.when(j > 0)
        def _():
            finish(j - 1)

    early = min(2, groups)
    pl.loop(0, early)(potential_group)
    if n > 2:
        chain_step(2)
    pl.loop(early, groups)(potential_group)
    finish(groups - 1)
    pot[a, q] = pfin[me]

    fbsend_rows = fpad.at[0:walks]
    fbsend_rows[...] = total
    for k in range(2):
        bias_out[k : k + 1, :] = fpad[pl.ds(k * every + me, 1), :]

    for t in range(3, n):
        chain_step(t)
    xbuf[s] = wbuf[parents[s]]
    xsend[...] = wbuf[parents[1 - s]]
    child_copy = remote(xsend, xbuf.at[s], ssem, (1,), sibling)
    child_copy.start()
    child_copy.wait_recv()
    eye = jnp.where(
        lax.broadcasted_iota(jnp.int32, (electrons, electrons), 0)
        == lax.broadcasted_iota(jnp.int32, (electrons, electrons), 1), 1.0, 0.0
    ).astype(BF16)
    term = lax.dot_general(
        xbuf[...].reshape(electrons, orbitals), eye, (((0,), (0,)), ((), ())), preferred_element_type=F32
    ).astype(BF16)
    summed = term.astype(F32)

    @pl.loop(0, groups)
    def _(j):
        for d, b in peers:
            pot_copy(d, b, j).wait_recv()

    for degree in range(1, TAYLOR + 1):
        product = jnp.dot(
            pot[...].reshape(n * padded, orbitals), term, preferred_element_type=F32
        )
        term = (product / jnp.float32(degree)).astype(BF16)
        if padded != rows:
            term = jnp.dot(layout, term, preferred_element_type=F32).astype(BF16)
        summed = summed + term.astype(F32)
    done[...] = lax.dot_general(
        eye, summed.astype(BF16), NT, preferred_element_type=F32
    ).astype(BF16).reshape(done.shape)
    last_copy = remote(done.at[1 - s], obuf.at[s], ssem, (2,), sibling)
    last_copy.start()
    obuf[s] = done[s]

    first_copy.wait_send()
    child_copy.wait_send()
    for copy in mixed_copies[0] + mixed_copies[1] + across_copies[0] + across_copies[1]:
        copy.wait_send()
    for copy in pick_copies + bias_copies:
        copy.wait_send()
    for t in range(n - 1):
        for way in range(2):
            @pl.when(chain_sends(way, t))
            def _():
                chain_copy(way, t).wait_send()

    @pl.loop(0, groups)
    def _(j):
        part_copy(j).wait_send()
        for d, b in peers:
            pot_copy(d, b, j).wait_send()

    last_copy.wait()
    walkers_out[...] = obuf[...]


def hand_over(walkers, bias, walkers_out, bias_out, sems):
    copies = [
        pltpu.make_async_copy(walkers, walkers_out, sems.at[0]),
        pltpu.make_async_copy(bias, bias_out, sems.at[1]),
    ]
    for copy in copies:
        copy.start()
    for copy in copies:
        copy.wait()


def shards(cholesky, trial_orbitals, walkers, intersection_inverse, noise_stream, offsets, parents):
    count, rows, orbitals = cholesky.shape
    walk_count, _, half = walkers.shape
    electrons = trial_orbitals.shape[1]
    n = lax.axis_size("pair")
    assert walk_count == 2 and lax.axis_size("sub") == 2 and count == LANES
    ways = lax.axis_size("rep")
    if walk_count * n * ways * GROUP > 1024:
        ways = 1
    every = n * ways
    groups = -(-rows // (GROUP * ways))
    span = groups * GROUP
    padded = span * ways
    walks = walk_count * every
    wide, deep = walks * GROUP, count * GROUP
    if padded != rows:
        cholesky = jnp.pad(cholesky, ((0, 0), (0, padded - rows), (0, 0)))

    vmem = pl.BlockSpec(memory_space=pltpu.VMEM)
    smem = pl.BlockSpec(memory_space=pltpu.SMEM)
    hbm = pl.BlockSpec(memory_space=pl.ANY)
    dma = pltpu.SemaphoreType.DMA
    new_walkers, force_bias = pl.pallas_call(
        functools.partial(step_kernel, n, ways, rows),
        out_shape=(
            jax.ShapeDtypeStruct((walk_count, half, orbitals), BF16),
            jax.ShapeDtypeStruct((walk_count, count), F32),
        ),
        in_specs=[hbm, hbm, hbm, hbm, hbm, smem, smem],
        out_specs=(vmem, vmem),
        scratch_shapes=[
            pltpu.VMEM((groups, count, GROUP, orbitals), BF16),
            pltpu.VMEM((2, half, orbitals), BF16),
            pltpu.VMEM((n, ways, span, electrons), BF16),
            pltpu.VMEM((2, every, span, electrons), BF16),
            pltpu.VMEM((walk_count * n, half, orbitals), BF16),
            pltpu.VMEM((2, every, GROUP, LANES), BF16),
            pltpu.VMEM((deep, wide), F32),
            pltpu.VMEM((count, deep), BF16),
            pltpu.VMEM((walks, count), F32),
            pltpu.VMEM((every, walks, count), F32),
            pltpu.VMEM((LANES, count), F32),
            pltpu.VMEM((walks // min(16, walks), min(16, walks) * GROUP, deep), BF16),
            pltpu.VMEM((walks, GROUP, orbitals), F32),
            pltpu.VMEM((groups, every, GROUP, orbitals), F32),
            pltpu.VMEM((groups, every, GROUP, orbitals), BF16),
            pltpu.VMEM((groups, every, GROUP, orbitals), BF16),
            pltpu.VMEM((every, span, orbitals), BF16),
            pltpu.VMEM((n, ways, span, orbitals), BF16),
            pltpu.VMEM((2, half, orbitals), BF16),
            pltpu.VMEM((half, orbitals), BF16),
            pltpu.VMEM((2, half, orbitals), BF16),
            pltpu.VMEM((2, half, orbitals), BF16),
            pltpu.VMEM((walk_count, GROUP, LANES), BF16),
            pltpu.VMEM((walks, 2 * LANES), F32),
            pltpu.VMEM((electrons, orbitals), BF16),
            pltpu.VMEM((walk_count, electrons, electrons), BF16),
            pltpu.VMEM((noise_stream.shape[0] // LANES, LANES), F32),
            dma((groups,)),
            dma((2, 3)),
            dma((2, 2, every)),
            dma((2, 2, every)),
            dma((2, 2, n)),
            dma((2, every)),
            dma((2, every)),
            dma((2, groups)),
            dma((2, every, groups)),
            dma((4,)),
        ],
        compiler_params=pltpu.CompilerParams(
            collective_id=0, has_side_effects=True, vmem_limit_bytes=58 * 1024 * 1024
        ),
    )(
        cholesky, trial_orbitals.T, intersection_inverse, jnp.swapaxes(walkers, 1, 2),
        noise_stream.reshape(-1, LANES), offsets, parents,
    )
    new_walkers, force_bias = pl.pallas_call(
        hand_over,
        out_shape=(
            jax.ShapeDtypeStruct(new_walkers.shape, BF16),
            jax.ShapeDtypeStruct(force_bias.shape, F32),
        ),
        in_specs=[hbm, hbm],
        out_specs=(hbm, hbm),
        scratch_shapes=[dma((2,))],
        compiler_params=pltpu.CompilerParams(vmem_limit_bytes=58 * 1024 * 1024),
    )(new_walkers, force_bias)
    return (jnp.swapaxes(new_walkers, 1, 2), force_bias)


def solution(mesh):
    in_specs = (
        P("sub", "pair", None),
        P(),
        P(("grp", "pair", "rep"), None, "sub"),
        P(("grp", "pair", "rep"), None, None),
        P("grp"),
        P("grp"),
        P(("grp", "pair", "rep")),
    )
    out_specs = (P(("grp", "pair", "rep"), None, "sub"), P(("grp", "pair", "rep"), "sub"))
    return jax.shard_map(shards, mesh=mesh, in_specs=in_specs, out_specs=out_specs, check_vma=False)
```

```python
import functools

import jax
import jax.numpy as jnp
from jax import lax
from jax.experimental import pallas as pl
from jax.experimental.pallas import tpu as pltpu
from jax.sharding import PartitionSpec as P

TAYLOR = 6
GROUP = 16
LANES = 128

field_scale = 1.6

MESH = pl.DeviceIdType.MESH
F32 = jnp.float32
BF16 = jnp.bfloat16
NT = (((1,), (1,)), ((), ()))


def step_kernel(
    n, ways, rows, chol, trial_in, inverse_in, walkers_in, noise_in, offsets, parents,
    walkers_out, bias_out,
    cbuf, wfirst, mixed, mixbuf, wbuf, rbuf, ybuf, ebuf, fbsend, fbbuf, fpad, kron, tmp, keep, psend, precv,
    pfin, pot, xbuf, xsend, done, picks, window, trial, inverse, noise,
    csem, ssem, msem, xsem, hsem, rsem, fsem, qsem, psem, isem,
):
    a = lax.axis_index("pair")
    s = lax.axis_index("sub")
    groups, count = cbuf.shape[0], cbuf.shape[1]
    electrons, orbitals = trial.shape
    every = n * ways
    q = lax.axis_index("rep") if ways > 1 else 0
    me = q * n + a
    span = groups * GROUP
    padded = span * ways
    walks = 2 * every
    wide = walks * GROUP
    deep = count * GROUP

    def chol_copy(j):
        return pltpu.make_async_copy(
            chol.at[:, pl.ds(pl.multiple_of(q * span + j * GROUP, GROUP), GROUP), :],
            cbuf.at[j], csem.at[j],
        )

    own_walkers = pl.ds(2 * a, 2)
    loads = [
        pltpu.make_async_copy(src, dst, isem.at[i])
        for i, (src, dst) in enumerate(
            [(walkers_in, wbuf.at[own_walkers]), (inverse_in, inverse), (noise_in, noise), (trial_in, trial)]
        )
    ]
    for load in loads:
        load.start()

    @pl.loop(0, groups)
    def _(j):
        chol_copy(j).start()

    peers = [(d, lax.rem(me + d, every)) for d in range(1, every)]

    def holder(c):
        return {"pair": lax.rem(c, n), "rep": lax.div(c, n)} if ways > 1 else {"pair": c}
    sibling = {"sub": 1 - s}

    def remote(src, dst, sems, place, target):
        return pltpu.make_async_remote_copy(
            src_ref=src, dst_ref=dst, send_sem=sems.at[(0,) + place], recv_sem=sems.at[(1,) + place],
            device_id=target, device_id_type=MESH,
        )

    spots = lax.broadcasted_iota(jnp.int32, (GROUP, LANES), 1)
    for k in range(2):
        column = lax.rem(parents[k], 2) * every + q * n + lax.div(parents[k], 2)
        picks[k] = jnp.where(spots == column, 1.0, 0.0).astype(BF16)

    barrier = pltpu.get_barrier_semaphore()
    pl.semaphore_signal(barrier, inc=1, device_id=sibling, device_id_type=MESH)
    for _, c in peers:
        pl.semaphore_signal(barrier, inc=1, device_id=holder(c), device_id_type=MESH)
    loads[0].wait()
    pl.semaphore_wait(barrier, every)

    first_copy = remote(wbuf.at[2 * a + 1 - s], wfirst.at[s], ssem, (0,), sibling)
    first_copy.start()
    pick_copies = [remote(picks, rbuf.at[:, me], rsem, (d,), holder(c)) for d, c in peers]
    for copy in pick_copies:
        copy.start()
    wfirst[s] = wbuf[2 * a + s]
    rbuf[:, me] = picks[...]
    loads[1].wait()
    loads[2].wait()
    if padded != rows:
        spot = lax.broadcasted_iota(jnp.int32, (orbitals, n * padded), 1)
        spot = jnp.where(spot % padded < rows, spot // padded * rows + spot % padded, -1)
        layout = jnp.where(
            spot == lax.broadcasted_iota(jnp.int32, (orbitals, n * padded), 0), 1.0, 0.0
        ).astype(BF16)
    first_copy.wait_recv()
    start = wfirst[...].reshape(electrons, orbitals)
    if padded != rows:
        start = jnp.dot(start, layout, preferred_element_type=F32).astype(BF16)
    mixed[...] = lax.dot_general(
        start, inverse[s], (((0,), (0,)), ((), ())), preferred_element_type=F32
    ).astype(BF16).reshape(n, ways, span, electrons)

    def chain_copy(way, t):
        block = a - t if way == 0 else a + t
        at = pl.ds(2 * block, 2)
        return remote(wbuf.at[at], wbuf.at[at], hsem, (way, t), {"pair": a + 1 - 2 * way})

    def chain_sends(way, t):
        return (a >= t) & (a + 1 < n) if way == 0 else (a + t < n) & (a > 0)

    def chain_gets(way, t):
        return a >= t + 1 if way == 0 else a + t + 1 < n

    def chain_step(t):
        for way in range(2):
            if t > 0:
                @pl.when(chain_gets(way, t - 1))
                def _():
                    back = a - t if way == 0 else a + t
                    at = pl.ds(2 * back, 2)
                    remote(
                        wbuf.at[at], wbuf.at[at], hsem, (way, t - 1), {"pair": a - 1 + 2 * way}
                    ).wait_recv()
            if t < n - 1:
                @pl.when(chain_sends(way, t))
                def _():
                    chain_copy(way, t).start()

    split = max(1, groups // 2)
    parts = [pl.ds(0, split * GROUP), pl.ds(split * GROUP, (groups - split) * GROUP)]
    mixed_copies = [
        [
            remote(
                mixed.at[lax.rem(c, n), lax.div(c, n), part], mixbuf.at[s, me, part], msem, (h, d), holder(c)
            )
            for d, c in peers
        ]
        for h, part in enumerate(parts)
    ]
    across_copies = [
        [
            remote(mixbuf.at[s, c, part], mixbuf.at[s, c, part], xsem, (h, d), sibling)
            for d, c in [(d, lax.rem(me + every - d, every)) for d in range(every)]
        ]
        for h, part in enumerate(parts)
    ]
    for h in range(2):
        for copy in mixed_copies[h]:
            copy.start()
    chain_step(0)
    mixbuf[s, me] = mixed[a, q]

    rep, rep_size = lax.axis_index("rep"), lax.axis_size("rep")
    low = jnp.zeros((walks, 2 * LANES), jnp.int32)
    number = lax.broadcasted_iota(jnp.int32, (walks, 2 * LANES), 0)
    for c in range(every):
        for k in range(2):
            home = c // n if ways > 1 else rep
            place = offsets[(c % n * rep_size + home) * 2 + k] + s * count
            row = lax.div(place, LANES)
            w = k * every + c
            window[w : w + 1, 0:LANES] = noise[pl.ds(row, 1), :]
            after = jnp.minimum(row + 1, noise.shape[0] - 1)
            window[w : w + 1, LANES:] = noise[pl.ds(after, 1), :]
            low = jnp.where(number == w, lax.rem(place, LANES), low)
    seen = window[...]
    amount = 1
    while amount < LANES:
        turned = jnp.concatenate([seen[:, amount:], seen[:, :amount]], axis=1)
        seen = jnp.where(lax.rem(lax.div(low, amount), 2) == 1, turned, seen)
        amount *= 2
    window[...] = seen

    ybuf[...] = jnp.zeros_like(ybuf)
    fpad[...] = jnp.zeros_like(fpad)
    ebuf[...] = jnp.where(
        lax.broadcasted_iota(jnp.int32, (count, deep), 1) // GROUP
        == lax.broadcasted_iota(jnp.int32, (count, deep), 0), 1.0, 0.0
    ).astype(BF16)

    def pass_across(h):
        across_copies[h][0].start()
        for copy, forward in zip(mixed_copies[h], across_copies[h][1:]):
            copy.wait_recv()
            forward.start()

    tile = max(GROUP, min(deep, 262144 // wide) // GROUP * GROUP)
    share = tile // GROUP

    def bias_group(j):
        chol_copy(j).wait()
        block_rows = mixbuf[:, :, pl.ds(pl.multiple_of(j * GROUP, GROUP), GROUP), :]
        density = jnp.dot(
            block_rows.reshape(wide, electrons), trial[...], preferred_element_type=F32
        ).astype(BF16)

        @pl.loop(0, deep // tile)
        def _(t):
            block = cbuf[j, pl.ds(t * share, share)].reshape(tile, orbitals)
            at = pl.ds(pl.multiple_of(t * tile, tile), tile)
            ybuf[at, :] += lax.dot_general(block, density, NT, preferred_element_type=F32)

    pass_across(0)
    for copy in across_copies[0]:
        copy.wait_recv()
    loads[3].wait()
    pl.loop(0, split - 1)(bias_group)
    pass_across(1)
    pl.loop(split - 1, split)(bias_group)
    for copy in across_copies[1]:
        copy.wait_recv()
    pl.loop(split, groups)(bias_group)

    same = (
        lax.broadcasted_iota(jnp.int32, (1, GROUP, wide), 1)
        == lax.broadcasted_iota(jnp.int32, (1, GROUP, wide), 2) % GROUP
    )
    traced = jnp.sum(jnp.where(same, ybuf[...].reshape(count, GROUP, wide), 0.0), axis=1)
    adder = jnp.where(
        lax.broadcasted_iota(jnp.int32, (walks, wide), 1) // GROUP
        == lax.broadcasted_iota(jnp.int32, (walks, wide), 0), 1.0, 0.0
    )
    partial = lax.dot_general(
        adder, traced, NT, preferred_element_type=F32, precision=lax.Precision.HIGHEST
    )
    fbsend[...] = partial
    fbbuf[me] = partial
    bias_copies = [remote(fbsend, fbbuf.at[me], fsem, (d,), holder(c)) for d, c in peers]
    for copy in bias_copies:
        copy.start()
    chain_step(1)
    for copy in pick_copies + bias_copies:
        copy.wait_recv()
    total = jnp.sum(fbbuf[...], axis=0)
    fpad[0:walks, :] = window[:, 0:LANES] - total
    fields = fpad[...].astype(BF16)

    some = min(16, walks)
    step = some * GROUP
    chunks = wide // step

    @pl.loop(0, chunks)
    def _(c):
        if chunks == 1:
            chosen = rbuf[...].reshape(step, LANES)
        else:
            per = every // some
            chosen = rbuf[c // per, pl.ds(lax.rem(c, per) * some, some)].reshape(step, LANES)
        spread = jnp.dot(chosen, fields, preferred_element_type=F32).astype(BF16)
        full = jnp.dot(spread, ebuf[...], preferred_element_type=F32)
        diagonal = (
            lax.broadcasted_iota(jnp.int32, (step, deep), 0) % GROUP
            == lax.broadcasted_iota(jnp.int32, (step, deep), 1) % GROUP
        )
        kron[c] = jnp.where(diagonal, full, 0.0).astype(BF16)

    def part_copy(j):
        return remote(psend.at[j], precv.at[j], qsem, (j,), sibling)

    def pot_copy(d, c, j):
        at = pl.ds(pl.multiple_of(j * GROUP, GROUP), GROUP)
        return remote(pfin.at[c, at], pot.at[a, q, at], psem, (d, j), holder(c))

    def finish(j):
        part_copy(j).wait_recv()
        at = pl.ds(pl.multiple_of(j * GROUP, GROUP), GROUP)
        pfin[:, at, :] = (field_scale * (keep[j] + precv[j].astype(F32))).astype(BF16)
        for d, b in peers:
            pot_copy(d, b, j).start()

    def potential_group(j):
        @pl.loop(0, chunks)
        def _(c):
            tmp[pl.ds(c * some, some)] = jnp.dot(
                kron[c], cbuf[j].reshape(deep, orbitals), preferred_element_type=F32
            ).reshape(some, GROUP, orbitals)

        psend[j] = tmp[pl.ds((1 - s) * every, every)].astype(BF16)
        part_copy(j).start()
        keep[j] = tmp[pl.ds(s * every, every)]

        @pl.when(j > 0)
        def _():
            finish(j - 1)

    pl.loop(0, groups)(potential_group)
    finish(groups - 1)
    if n > 2:
        chain_step(2)
    pot[a, q] = pfin[me]

    fbsend_rows = fpad.at[0:walks]
    fbsend_rows[...] = total
    for k in range(2):
        bias_out[k : k + 1, :] = fpad[pl.ds(k * every + me, 1), :]

    for t in range(3, n):
        chain_step(t)
    xbuf[s] = wbuf[parents[s]]
    xsend[...] = wbuf[parents[1 - s]]
    child_copy = remote(xsend, xbuf.at[s], ssem, (1,), sibling)
    child_copy.start()
    child_copy.wait_recv()
    eye = jnp.where(
        lax.broadcasted_iota(jnp.int32, (electrons, electrons), 0)
        == lax.broadcasted_iota(jnp.int32, (electrons, electrons), 1), 1.0, 0.0
    ).astype(BF16)
    term = lax.dot_general(
        xbuf[...].reshape(electrons, orbitals), eye, (((0,), (0,)), ((), ())), preferred_element_type=F32
    ).astype(BF16)
    summed = term.astype(F32)

    @pl.loop(0, groups)
    def _(j):
        for d, b in peers:
            pot_copy(d, b, j).wait_recv()

    for degree in range(1, TAYLOR + 1):
        product = jnp.dot(
            pot[...].reshape(n * padded, orbitals), term, preferred_element_type=F32
        )
        term = (product / jnp.float32(degree)).astype(BF16)
        if padded != rows:
            term = jnp.dot(layout, term, preferred_element_type=F32).astype(BF16)
        summed = summed + term.astype(F32)
    done[...] = lax.dot_general(
        eye, summed.astype(BF16), NT, preferred_element_type=F32
    ).astype(BF16).reshape(done.shape)
    last_copy = remote(done.at[1 - s], walkers_out.at[s], ssem, (2,), sibling)
    last_copy.start()
    walkers_out[s] = done[s]

    first_copy.wait_send()
    child_copy.wait_send()
    for copy in mixed_copies[0] + mixed_copies[1] + across_copies[0] + across_copies[1]:
        copy.wait_send()
    for copy in pick_copies + bias_copies:
        copy.wait_send()
    for t in range(n - 1):
        for way in range(2):
            @pl.when(chain_sends(way, t))
            def _():
                chain_copy(way, t).wait_send()

    @pl.loop(0, groups)
    def _(j):
        part_copy(j).wait_send()
        for d, b in peers:
            pot_copy(d, b, j).wait_send()

    last_copy.wait()


def shards(cholesky, trial_orbitals, walkers, intersection_inverse, noise_stream, offsets, parents):
    count, rows, orbitals = cholesky.shape
    walk_count, _, half = walkers.shape
    electrons = trial_orbitals.shape[1]
    n = lax.axis_size("pair")
    assert walk_count == 2 and lax.axis_size("sub") == 2 and count == LANES
    ways = lax.axis_size("rep")
    if walk_count * n * ways * GROUP > 1024:
        ways = 1
    every = n * ways
    groups = -(-rows // (GROUP * ways))
    span = groups * GROUP
    padded = span * ways
    walks = walk_count * every
    wide, deep = walks * GROUP, count * GROUP
    if padded != rows:
        cholesky = jnp.pad(cholesky, ((0, 0), (0, padded - rows), (0, 0)))

    vmem = pl.BlockSpec(memory_space=pltpu.VMEM)
    smem = pl.BlockSpec(memory_space=pltpu.SMEM)
    hbm = pl.BlockSpec(memory_space=pl.ANY)
    dma = pltpu.SemaphoreType.DMA
    new_walkers, force_bias = pl.pallas_call(
        functools.partial(step_kernel, n, ways, rows),
        out_shape=(
            jax.ShapeDtypeStruct((walk_count, half, orbitals), BF16),
            jax.ShapeDtypeStruct((walk_count, count), F32),
        ),
        in_specs=[hbm, hbm, hbm, hbm, hbm, smem, smem],
        out_specs=(vmem, vmem),
        scratch_shapes=[
            pltpu.VMEM((groups, count, GROUP, orbitals), BF16),
            pltpu.VMEM((2, half, orbitals), BF16),
            pltpu.VMEM((n, ways, span, electrons), BF16),
            pltpu.VMEM((2, every, span, electrons), BF16),
            pltpu.VMEM((walk_count * n, half, orbitals), BF16),
            pltpu.VMEM((2, every, GROUP, LANES), BF16),
            pltpu.VMEM((deep, wide), F32),
            pltpu.VMEM((count, deep), BF16),
            pltpu.VMEM((walks, count), F32),
            pltpu.VMEM((every, walks, count), F32),
            pltpu.VMEM((LANES, count), F32),
            pltpu.VMEM((walks // min(16, walks), min(16, walks) * GROUP, deep), BF16),
            pltpu.VMEM((walks, GROUP, orbitals), F32),
            pltpu.VMEM((groups, every, GROUP, orbitals), F32),
            pltpu.VMEM((groups, every, GROUP, orbitals), BF16),
            pltpu.VMEM((groups, every, GROUP, orbitals), BF16),
            pltpu.VMEM((every, span, orbitals), BF16),
            pltpu.VMEM((n, ways, span, orbitals), BF16),
            pltpu.VMEM((2, half, orbitals), BF16),
            pltpu.VMEM((half, orbitals), BF16),
            pltpu.VMEM((2, half, orbitals), BF16),
            pltpu.VMEM((walk_count, GROUP, LANES), BF16),
            pltpu.VMEM((walks, 2 * LANES), F32),
            pltpu.VMEM((electrons, orbitals), BF16),
            pltpu.VMEM((walk_count, electrons, electrons), BF16),
            pltpu.VMEM((noise_stream.shape[0] // LANES, LANES), F32),
            dma((groups,)),
            dma((2, 3)),
            dma((2, 2, every)),
            dma((2, 2, every)),
            dma((2, 2, n)),
            dma((2, every)),
            dma((2, every)),
            dma((2, groups)),
            dma((2, every, groups)),
            dma((4,)),
        ],
        compiler_params=pltpu.CompilerParams(
            collective_id=0, has_side_effects=True, vmem_limit_bytes=58 * 1024 * 1024
        ),
    )(
        cholesky, trial_orbitals.T, intersection_inverse, jnp.swapaxes(walkers, 1, 2),
        noise_stream.reshape(-1, LANES), offsets, parents,
    )
    return (jnp.swapaxes(new_walkers, 1, 2), force_bias)


def solution(mesh):
    in_specs = (
        P("sub", "pair", None),
        P(),
        P(("grp", "pair", "rep"), None, "sub"),
        P(("grp", "pair", "rep"), None, None),
        P("grp"),
        P("grp"),
        P(("grp", "pair", "rep")),
    )
    out_specs = (P(("grp", "pair", "rep"), None, "sub"), P(("grp", "pair", "rep"), "sub"))
    return jax.shard_map(shards, mesh=mesh, in_specs=in_specs, out_specs=out_specs, check_vma=False)
```

```python
import functools

import jax
import jax.numpy as jnp
from jax import lax
from jax.experimental import pallas as pl
from jax.experimental.pallas import tpu as pltpu
from jax.sharding import PartitionSpec as P

TAYLOR = 6
GROUP = 16
LANES = 128

field_scale = 1.6

MESH = pl.DeviceIdType.MESH
F32 = jnp.float32
BF16 = jnp.bfloat16
NT = (((1,), (1,)), ((), ()))


def mixed_rows(groups, electrons):
    split = max(1, groups // 2)
    packed = electrons == LANES + LANES // 2
    places, row, starts = [], 0, []
    for low, high in ((0, split), (split, groups)):
        starts.append(row)
        tails = row + (high - low) * GROUP
        for i in range(high - low):
            places.append((row + i * GROUP, tails + i // 2 * GROUP, i % 2))
        row = tails + (-(-(high - low) // 2) * GROUP if packed else 0)
    return places, starts[1], row, packed, LANES if packed else electrons


def step_kernel(
    n, ways, rows, chol, trial_in, inverse_in, walkers_in, noise_in, offsets, parents,
    walkers_out, bias_out,
    cbuf, wfirst, mixed, mixbuf, wbuf, rbuf, ybuf, ebuf, fbsend, fbbuf, fpad, kron, tmp, keep, psend, precv,
    pfin, pot, xbuf, xsend, done, picks, window, trial, inverse, noise,
    csem, ssem, msem, xsem, hsem, rsem, fsem, qsem, psem, isem,
):
    a = lax.axis_index("pair")
    s = lax.axis_index("sub")
    groups, count = cbuf.shape[0], cbuf.shape[1]
    electrons, orbitals = trial.shape
    every = n * ways
    q = lax.axis_index("rep") if ways > 1 else 0
    me = q * n + a
    span = groups * GROUP
    padded = span * ways
    walks = 2 * every
    wide = walks * GROUP
    deep = count * GROUP

    def chol_copy(j):
        return pltpu.make_async_copy(
            chol.at[:, pl.ds(pl.multiple_of(q * span + j * GROUP, GROUP), GROUP), :],
            cbuf.at[j], csem.at[j],
        )

    own_walkers = pl.ds(2 * a, 2)
    loads = [
        pltpu.make_async_copy(src, dst, isem.at[i])
        for i, (src, dst) in enumerate(
            [(walkers_in, wbuf.at[own_walkers]), (inverse_in, inverse), (noise_in, noise), (trial_in, trial)]
        )
    ]
    for load in loads:
        load.start()

    @pl.loop(0, groups)
    def _(j):
        chol_copy(j).start()

    peers = [(d, lax.rem(me + d, every)) for d in range(1, every)]

    def holder(c):
        return {"pair": lax.rem(c, n), "rep": lax.div(c, n)} if ways > 1 else {"pair": c}
    sibling = {"sub": 1 - s}

    def remote(src, dst, sems, place, target):
        return pltpu.make_async_remote_copy(
            src_ref=src, dst_ref=dst, send_sem=sems.at[(0,) + place], recv_sem=sems.at[(1,) + place],
            device_id=target, device_id_type=MESH,
        )

    spots = lax.broadcasted_iota(jnp.int32, (GROUP, LANES), 1)
    for k in range(2):
        column = lax.rem(parents[k], 2) * every + q * n + lax.div(parents[k], 2)
        picks[k] = jnp.where(spots == column, 1.0, 0.0).astype(BF16)

    barrier = pltpu.get_barrier_semaphore()
    pl.semaphore_signal(barrier, inc=1, device_id=sibling, device_id_type=MESH)
    for _, c in peers:
        pl.semaphore_signal(barrier, inc=1, device_id=holder(c), device_id_type=MESH)
    loads[0].wait()
    pl.semaphore_wait(barrier, every)

    first_copy = remote(wbuf.at[2 * a + 1 - s], wfirst.at[s], ssem, (0,), sibling)
    first_copy.start()
    pick_copies = [remote(picks, rbuf.at[:, me], rsem, (d,), holder(c)) for d, c in peers]
    for copy in pick_copies:
        copy.start()
    wfirst[s] = wbuf[2 * a + s]
    rbuf[:, me] = picks[...]
    loads[1].wait()
    loads[2].wait()
    if padded != rows:
        spot = lax.broadcasted_iota(jnp.int32, (orbitals, n * padded), 1)
        spot = jnp.where(spot % padded < rows, spot // padded * rows + spot % padded, -1)
        layout = jnp.where(
            spot == lax.broadcasted_iota(jnp.int32, (orbitals, n * padded), 0), 1.0, 0.0
        ).astype(BF16)
    first_copy.wait_recv()
    start = wfirst[...].reshape(electrons, orbitals)
    if padded != rows:
        start = jnp.dot(start, layout, preferred_element_type=F32).astype(BF16)
    product = lax.dot_general(
        start, inverse[s], (((0,), (0,)), ((), ())), preferred_element_type=F32
    ).astype(BF16).reshape(n, ways, span, electrons)
    places, cut, sent, packed, width = mixed_rows(groups, electrons)
    for j, (first, tail, second) in enumerate(places):
        rows_of = product[:, :, j * GROUP : (j + 1) * GROUP, :]
        mixed[:, :, first : first + GROUP, :] = rows_of[..., :width]
        if packed and not second:
            beside = (
                product[:, :, (j + 1) * GROUP : (j + 2) * GROUP, width:]
                if j + 1 < groups and places[j + 1][2]
                else jnp.zeros_like(rows_of[..., width:])
            )
            mixed[:, :, tail : tail + GROUP, :] = jnp.concatenate([rows_of[..., width:], beside], axis=-1)

    def chain_copy(way, t):
        block = a - t if way == 0 else a + t
        at = pl.ds(2 * block, 2)
        return remote(wbuf.at[at], wbuf.at[at], hsem, (way, t), {"pair": a + 1 - 2 * way})

    def chain_sends(way, t):
        return (a >= t) & (a + 1 < n) if way == 0 else (a + t < n) & (a > 0)

    def chain_gets(way, t):
        return a >= t + 1 if way == 0 else a + t + 1 < n

    def chain_step(t):
        for way in range(2):
            if t > 0:
                @pl.when(chain_gets(way, t - 1))
                def _():
                    back = a - t if way == 0 else a + t
                    at = pl.ds(2 * back, 2)
                    remote(
                        wbuf.at[at], wbuf.at[at], hsem, (way, t - 1), {"pair": a - 1 + 2 * way}
                    ).wait_recv()
            if t < n - 1:
                @pl.when(chain_sends(way, t))
                def _():
                    chain_copy(way, t).start()

    split = max(1, groups // 2)
    parts = [pl.ds(0, cut), pl.ds(cut, sent - cut)]
    mixed_copies = [
        [
            remote(
                mixed.at[lax.rem(c, n), lax.div(c, n), part], mixbuf.at[s, me, part], msem, (h, d), holder(c)
            )
            for d, c in peers
        ]
        for h, part in enumerate(parts)
    ]
    across_copies = [
        [
            remote(mixbuf.at[s, c, part], mixbuf.at[s, c, part], xsem, (h, d), sibling)
            for d, c in [(d, lax.rem(me + every - d, every)) for d in range(every)]
        ]
        for h, part in enumerate(parts)
    ]
    for h in range(2):
        for copy in mixed_copies[h]:
            copy.start()
    chain_step(0)
    mixbuf[s, me] = mixed[a, q]

    rep, rep_size = lax.axis_index("rep"), lax.axis_size("rep")
    low = jnp.zeros((walks, 2 * LANES), jnp.int32)
    number = lax.broadcasted_iota(jnp.int32, (walks, 2 * LANES), 0)
    for c in range(every):
        for k in range(2):
            home = c // n if ways > 1 else rep
            place = offsets[(c % n * rep_size + home) * 2 + k] + s * count
            row = lax.div(place, LANES)
            w = k * every + c
            window[w : w + 1, 0:LANES] = noise[pl.ds(row, 1), :]
            after = jnp.minimum(row + 1, noise.shape[0] - 1)
            window[w : w + 1, LANES:] = noise[pl.ds(after, 1), :]
            low = jnp.where(number == w, lax.rem(place, LANES), low)
    seen = window[...]
    amount = 1
    while amount < LANES:
        turned = jnp.concatenate([seen[:, amount:], seen[:, :amount]], axis=1)
        seen = jnp.where(lax.rem(lax.div(low, amount), 2) == 1, turned, seen)
        amount *= 2
    window[...] = seen

    ybuf[...] = jnp.zeros_like(ybuf)
    fpad[...] = jnp.zeros_like(fpad)
    ebuf[...] = jnp.where(
        lax.broadcasted_iota(jnp.int32, (count, deep), 1) // GROUP
        == lax.broadcasted_iota(jnp.int32, (count, deep), 0), 1.0, 0.0
    ).astype(BF16)

    def pass_across(h):
        across_copies[h][0].start()
        for copy, forward in zip(mixed_copies[h], across_copies[h][1:]):
            copy.wait_recv()
            forward.start()

    tile = max(GROUP, min(deep, 262144 // wide) // GROUP * GROUP)
    share = tile // GROUP

    def bias_group(j):
        chol_copy(j).wait()
        first, tail, second = places[j]
        block_rows = mixbuf[:, :, first : first + GROUP, :].reshape(wide, width)
        if packed:
            ends = mixbuf[:, :, tail : tail + GROUP, :].reshape(wide, width)
            half = electrons - width
            ends = ends[:, half:] if second else ends[:, :half]
            block_rows = jnp.concatenate([block_rows, ends], axis=1)
        density = jnp.dot(block_rows, trial[...], preferred_element_type=F32).astype(BF16)

        @pl.loop(0, deep // tile)
        def _(t):
            block = cbuf[j, pl.ds(t * share, share)].reshape(tile, orbitals)
            at = pl.ds(pl.multiple_of(t * tile, tile), tile)
            ybuf[at, :] += lax.dot_general(block, density, NT, preferred_element_type=F32)

    pass_across(0)
    for copy in across_copies[0]:
        copy.wait_recv()
    loads[3].wait()
    for j in range(split - 1):
        bias_group(j)
    pass_across(1)
    bias_group(split - 1)
    for copy in across_copies[1]:
        copy.wait_recv()
    for j in range(split, groups):
        bias_group(j)

    same = (
        lax.broadcasted_iota(jnp.int32, (1, GROUP, wide), 1)
        == lax.broadcasted_iota(jnp.int32, (1, GROUP, wide), 2) % GROUP
    )
    traced = jnp.sum(jnp.where(same, ybuf[...].reshape(count, GROUP, wide), 0.0), axis=1)
    adder = jnp.where(
        lax.broadcasted_iota(jnp.int32, (walks, wide), 1) // GROUP
        == lax.broadcasted_iota(jnp.int32, (walks, wide), 0), 1.0, 0.0
    )
    partial = lax.dot_general(
        adder, traced, NT, preferred_element_type=F32, precision=lax.Precision.HIGHEST
    )
    fbsend[...] = partial
    fbbuf[me] = partial
    bias_copies = [remote(fbsend, fbbuf.at[me], fsem, (d,), holder(c)) for d, c in peers]
    for copy in bias_copies:
        copy.start()
    chain_step(1)
    for copy in pick_copies + bias_copies:
        copy.wait_recv()
    total = jnp.sum(fbbuf[...], axis=0)
    fpad[0:walks, :] = window[:, 0:LANES] - total
    fields = fpad[...].astype(BF16)

    some = min(16, walks)
    step = some * GROUP
    chunks = wide // step

    @pl.loop(0, chunks)
    def _(c):
        if chunks == 1:
            chosen = rbuf[...].reshape(step, LANES)
        else:
            per = every // some
            chosen = rbuf[c // per, pl.ds(lax.rem(c, per) * some, some)].reshape(step, LANES)
        spread = jnp.dot(chosen, fields, preferred_element_type=F32).astype(BF16)
        full = jnp.dot(spread, ebuf[...], preferred_element_type=F32)
        diagonal = (
            lax.broadcasted_iota(jnp.int32, (step, deep), 0) % GROUP
            == lax.broadcasted_iota(jnp.int32, (step, deep), 1) % GROUP
        )
        kron[c] = jnp.where(diagonal, full, 0.0).astype(BF16)

    def part_copy(j):
        return remote(psend.at[j], precv.at[j], qsem, (j,), sibling)

    def pot_copy(d, c, j):
        at = pl.ds(pl.multiple_of(j * GROUP, GROUP), GROUP)
        return remote(pfin.at[c, at], pot.at[a, q, at], psem, (d, j), holder(c))

    def finish(j):
        part_copy(j).wait_recv()
        at = pl.ds(pl.multiple_of(j * GROUP, GROUP), GROUP)
        pfin[:, at, :] = (field_scale * (keep[j] + precv[j].astype(F32))).astype(BF16)
        for d, b in peers:
            pot_copy(d, b, j).start()

    def potential_group(j):
        @pl.loop(0, chunks)
        def _(c):
            tmp[pl.ds(c * some, some)] = jnp.dot(
                kron[c], cbuf[j].reshape(deep, orbitals), preferred_element_type=F32
            ).reshape(some, GROUP, orbitals)

        psend[j] = tmp[pl.ds((1 - s) * every, every)].astype(BF16)
        part_copy(j).start()
        keep[j] = tmp[pl.ds(s * every, every)]

        @pl.when(j > 0)
        def _():
            finish(j - 1)

    pl.loop(0, groups)(potential_group)
    finish(groups - 1)
    if n > 2:
        chain_step(2)
    pot[a, q] = pfin[me]

    fbsend_rows = fpad.at[0:walks]
    fbsend_rows[...] = total
    for k in range(2):
        bias_out[k : k + 1, :] = fpad[pl.ds(k * every + me, 1), :]

    for t in range(3, n):
        chain_step(t)
    xbuf[s] = wbuf[parents[s]]
    xsend[...] = wbuf[parents[1 - s]]
    child_copy = remote(xsend, xbuf.at[s], ssem, (1,), sibling)
    child_copy.start()
    child_copy.wait_recv()
    eye = jnp.where(
        lax.broadcasted_iota(jnp.int32, (electrons, electrons), 0)
        == lax.broadcasted_iota(jnp.int32, (electrons, electrons), 1), 1.0, 0.0
    ).astype(BF16)
    term = lax.dot_general(
        xbuf[...].reshape(electrons, orbitals), eye, (((0,), (0,)), ((), ())), preferred_element_type=F32
    ).astype(BF16)
    summed = term.astype(F32)

    @pl.loop(0, groups)
    def _(j):
        for d, b in peers:
            pot_copy(d, b, j).wait_recv()

    for degree in range(1, TAYLOR + 1):
        product = jnp.dot(
            pot[...].reshape(n * padded, orbitals), term, preferred_element_type=F32
        )
        term = (product * jnp.float32(1.0 / degree)).astype(BF16)
        if padded != rows:
            term = jnp.dot(layout, term, preferred_element_type=F32).astype(BF16)
        summed = summed + term.astype(F32)
    done[...] = lax.dot_general(
        eye, summed.astype(BF16), NT, preferred_element_type=F32
    ).astype(BF16).reshape(done.shape)
    last_copy = remote(done.at[1 - s], walkers_out.at[s], ssem, (2,), sibling)
    last_copy.start()
    walkers_out[s] = done[s]

    first_copy.wait_send()
    child_copy.wait_send()
    for copy in mixed_copies[0] + mixed_copies[1] + across_copies[0] + across_copies[1]:
        copy.wait_send()
    for copy in pick_copies + bias_copies:
        copy.wait_send()
    for t in range(n - 1):
        for way in range(2):
            @pl.when(chain_sends(way, t))
            def _():
                chain_copy(way, t).wait_send()

    @pl.loop(0, groups)
    def _(j):
        part_copy(j).wait_send()
        for d, b in peers:
            pot_copy(d, b, j).wait_send()

    last_copy.wait()


def shards(cholesky, trial_orbitals, walkers, intersection_inverse, noise_stream, offsets, parents):
    count, rows, orbitals = cholesky.shape
    walk_count, _, half = walkers.shape
    electrons = trial_orbitals.shape[1]
    n = lax.axis_size("pair")
    assert walk_count == 2 and lax.axis_size("sub") == 2 and count == LANES
    ways = lax.axis_size("rep")
    if walk_count * n * ways * GROUP > 1024:
        ways = 1
    every = n * ways
    groups = -(-rows // (GROUP * ways))
    span = groups * GROUP
    padded = span * ways
    walks = walk_count * every
    _, _, sent, _, width = mixed_rows(groups, electrons)
    wide, deep = walks * GROUP, count * GROUP
    if padded != rows:
        cholesky = jnp.pad(cholesky, ((0, 0), (0, padded - rows), (0, 0)))

    vmem = pl.BlockSpec(memory_space=pltpu.VMEM)
    smem = pl.BlockSpec(memory_space=pltpu.SMEM)
    hbm = pl.BlockSpec(memory_space=pl.ANY)
    dma = pltpu.SemaphoreType.DMA
    new_walkers, force_bias = pl.pallas_call(
        functools.partial(step_kernel, n, ways, rows),
        out_shape=(
            jax.ShapeDtypeStruct((walk_count, half, orbitals), BF16),
            jax.ShapeDtypeStruct((walk_count, count), F32),
        ),
        in_specs=[hbm, hbm, hbm, hbm, hbm, smem, smem],
        out_specs=(vmem, vmem),
        scratch_shapes=[
            pltpu.VMEM((groups, count, GROUP, orbitals), BF16),
            pltpu.VMEM((2, half, orbitals), BF16),
            pltpu.VMEM((n, ways, sent, width), BF16),
            pltpu.VMEM((2, every, sent, width), BF16),
            pltpu.VMEM((walk_count * n, half, orbitals), BF16),
            pltpu.VMEM((2, every, GROUP, LANES), BF16),
            pltpu.VMEM((deep, wide), F32),
            pltpu.VMEM((count, deep), BF16),
            pltpu.VMEM((walks, count), F32),
            pltpu.VMEM((every, walks, count), F32),
            pltpu.VMEM((LANES, count), F32),
            pltpu.VMEM((walks // min(16, walks), min(16, walks) * GROUP, deep), BF16),
            pltpu.VMEM((walks, GROUP, orbitals), F32),
            pltpu.VMEM((groups, every, GROUP, orbitals), F32),
            pltpu.VMEM((groups, every, GROUP, orbitals), BF16),
            pltpu.VMEM((groups, every, GROUP, orbitals), BF16),
            pltpu.VMEM((every, span, orbitals), BF16),
            pltpu.VMEM((n, ways, span, orbitals), BF16),
            pltpu.VMEM((2, half, orbitals), BF16),
            pltpu.VMEM((half, orbitals), BF16),
            pltpu.VMEM((2, half, orbitals), BF16),
            pltpu.VMEM((walk_count, GROUP, LANES), BF16),
            pltpu.VMEM((walks, 2 * LANES), F32),
            pltpu.VMEM((electrons, orbitals), BF16),
            pltpu.VMEM((walk_count, electrons, electrons), BF16),
            pltpu.VMEM((noise_stream.shape[0] // LANES, LANES), F32),
            dma((groups,)),
            dma((2, 3)),
            dma((2, 2, every)),
            dma((2, 2, every)),
            dma((2, 2, n)),
            dma((2, every)),
            dma((2, every)),
            dma((2, groups)),
            dma((2, every, groups)),
            dma((4,)),
        ],
        compiler_params=pltpu.CompilerParams(
            collective_id=0, has_side_effects=True, vmem_limit_bytes=58 * 1024 * 1024
        ),
    )(
        cholesky, trial_orbitals.T, intersection_inverse, jnp.swapaxes(walkers, 1, 2),
        noise_stream.reshape(-1, LANES), offsets, parents,
    )
    return (jnp.swapaxes(new_walkers, 1, 2), force_bias)


def solution(mesh):
    in_specs = (
        P("sub", "pair", None),
        P(),
        P(("grp", "pair", "rep"), None, "sub"),
        P(("grp", "pair", "rep"), None, None),
        P("grp"),
        P("grp"),
        P(("grp", "pair", "rep")),
    )
    out_specs = (P(("grp", "pair", "rep"), None, "sub"), P(("grp", "pair", "rep"), "sub"))
    return jax.shard_map(shards, mesh=mesh, in_specs=in_specs, out_specs=out_specs, check_vma=False)
```

```python
import functools

import jax
import jax.numpy as jnp
from jax import lax
from jax.experimental import pallas as pl
from jax.experimental.pallas import tpu as pltpu
from jax.sharding import PartitionSpec as P

TAYLOR = 6
GROUP = 16
LANES = 128

field_scale = 1.6

MESH = pl.DeviceIdType.MESH
F32 = jnp.float32
BF16 = jnp.bfloat16
NT = (((1,), (1,)), ((), ()))


def mixed_rows(groups, electrons):
    split = max(1, groups // 2)
    packed = electrons == LANES + LANES // 2
    places, row, starts = [], 0, []
    for low, high in ((0, split), (split, groups)):
        starts.append(row)
        tails = row + (high - low) * GROUP
        for i in range(high - low):
            places.append((row + i * GROUP, tails + i // 2 * GROUP, i % 2))
        row = tails + (-(-(high - low) // 2) * GROUP if packed else 0)
    return places, starts[1], row, packed, LANES if packed else electrons


def step_kernel(
    n, ways, rows, chol, trial_in, inverse_in, walkers_in, noise_in, offsets, parents,
    walkers_out, bias_out,
    cbuf, wfirst, mixed, mixbuf, wbuf, rbuf, ybuf, ebuf, fbsend, fbbuf, fpad, kron, tmp, keep, psend, precv,
    pfin, pot, xbuf, xsend, done, picks, window, trial, inverse, noise, biasbuf,
    csem, ssem, msem, xsem, hsem, rsem, fsem, qsem, psem, isem,
):
    a = lax.axis_index("pair")
    s = lax.axis_index("sub")
    groups, count = cbuf.shape[0], cbuf.shape[1]
    electrons, orbitals = trial.shape
    every = n * ways
    q = lax.axis_index("rep") if ways > 1 else 0
    me = q * n + a
    span = groups * GROUP
    padded = span * ways
    walks = 2 * every
    wide = walks * GROUP
    deep = count * GROUP

    def chol_copy(j):
        return pltpu.make_async_copy(
            chol.at[:, pl.ds(pl.multiple_of(q * span + j * GROUP, GROUP), GROUP), :],
            cbuf.at[j], csem.at[j],
        )

    own_walkers = pl.ds(2 * a, 2)
    loads = [
        pltpu.make_async_copy(src, dst, isem.at[i])
        for i, (src, dst) in enumerate(
            [(walkers_in, wbuf.at[own_walkers]), (inverse_in, inverse), (noise_in, noise), (trial_in, trial)]
        )
    ]
    for load in loads:
        load.start()

    @pl.loop(0, groups)
    def _(j):
        chol_copy(j).start()

    peers = [(d, lax.rem(me + d, every)) for d in range(1, every)]

    def holder(c):
        return {"pair": lax.rem(c, n), "rep": lax.div(c, n)} if ways > 1 else {"pair": c}
    sibling = {"sub": 1 - s}

    def remote(src, dst, sems, place, target):
        return pltpu.make_async_remote_copy(
            src_ref=src, dst_ref=dst, send_sem=sems.at[(0,) + place], recv_sem=sems.at[(1,) + place],
            device_id=target, device_id_type=MESH,
        )

    spots = lax.broadcasted_iota(jnp.int32, (GROUP, LANES), 1)
    for k in range(2):
        column = lax.rem(parents[k], 2) * every + q * n + lax.div(parents[k], 2)
        picks[k] = jnp.where(spots == column, 1.0, 0.0).astype(BF16)

    barrier = pltpu.get_barrier_semaphore()
    pl.semaphore_signal(barrier, inc=1, device_id=sibling, device_id_type=MESH)
    for _, c in peers:
        pl.semaphore_signal(barrier, inc=1, device_id=holder(c), device_id_type=MESH)
    loads[0].wait()
    pl.semaphore_wait(barrier, every)

    first_copy = remote(wbuf.at[2 * a + 1 - s], wfirst.at[s], ssem, (0,), sibling)
    first_copy.start()
    pick_copies = [remote(picks, rbuf.at[:, me], rsem, (d,), holder(c)) for d, c in peers]
    for copy in pick_copies:
        copy.start()
    wfirst[s] = wbuf[2 * a + s]
    rbuf[:, me] = picks[...]
    loads[1].wait()
    loads[2].wait()
    if padded != rows:
        spot = lax.broadcasted_iota(jnp.int32, (orbitals, n * padded), 1)
        spot = jnp.where(spot % padded < rows, spot // padded * rows + spot % padded, -1)
        layout = jnp.where(
            spot == lax.broadcasted_iota(jnp.int32, (orbitals, n * padded), 0), 1.0, 0.0
        ).astype(BF16)
    first_copy.wait_recv()
    start = wfirst[...].reshape(electrons, orbitals)
    if padded != rows:
        start = jnp.dot(start, layout, preferred_element_type=F32).astype(BF16)
    product = lax.dot_general(
        start, inverse[s], (((0,), (0,)), ((), ())), preferred_element_type=F32
    ).astype(BF16).reshape(n, ways, span, electrons)
    places, cut, sent, packed, width = mixed_rows(groups, electrons)
    for j, (first, tail, second) in enumerate(places):
        rows_of = product[:, :, j * GROUP : (j + 1) * GROUP, :]
        mixed[:, :, first : first + GROUP, :] = rows_of[..., :width]
        if packed and not second:
            beside = (
                product[:, :, (j + 1) * GROUP : (j + 2) * GROUP, width:]
                if j + 1 < groups and places[j + 1][2]
                else jnp.zeros_like(rows_of[..., width:])
            )
            mixed[:, :, tail : tail + GROUP, :] = jnp.concatenate([rows_of[..., width:], beside], axis=-1)

    def chain_copy(way, t):
        block = a - t if way == 0 else a + t
        at = pl.ds(2 * block, 2)
        return remote(wbuf.at[at], wbuf.at[at], hsem, (way, t), {"pair": a + 1 - 2 * way})

    def chain_sends(way, t):
        return (a >= t) & (a + 1 < n) if way == 0 else (a + t < n) & (a > 0)

    def chain_gets(way, t):
        return a >= t + 1 if way == 0 else a + t + 1 < n

    def chain_step(t):
        for way in range(2):
            if t > 0:
                @pl.when(chain_gets(way, t - 1))
                def _():
                    back = a - t if way == 0 else a + t
                    at = pl.ds(2 * back, 2)
                    remote(
                        wbuf.at[at], wbuf.at[at], hsem, (way, t - 1), {"pair": a - 1 + 2 * way}
                    ).wait_recv()
            if t < n - 1:
                @pl.when(chain_sends(way, t))
                def _():
                    chain_copy(way, t).start()

    split = max(1, groups // 2)
    parts = [pl.ds(0, cut), pl.ds(cut, sent - cut)]
    mixed_copies = [
        [
            remote(
                mixed.at[lax.rem(c, n), lax.div(c, n), part], mixbuf.at[s, me, part], msem, (h, d), holder(c)
            )
            for d, c in peers
        ]
        for h, part in enumerate(parts)
    ]
    across_copies = [
        [
            remote(mixbuf.at[s, c, part], mixbuf.at[s, c, part], xsem, (h, d), sibling)
            for d, c in [(d, lax.rem(me + every - d, every)) for d in range(every)]
        ]
        for h, part in enumerate(parts)
    ]
    for h in range(2):
        for copy in mixed_copies[h]:
            copy.start()
    chain_step(0)
    mixbuf[s, me] = mixed[a, q]

    rep, rep_size = lax.axis_index("rep"), lax.axis_size("rep")
    low = jnp.zeros((walks, 2 * LANES), jnp.int32)
    number = lax.broadcasted_iota(jnp.int32, (walks, 2 * LANES), 0)
    for c in range(every):
        for k in range(2):
            home = c // n if ways > 1 else rep
            place = offsets[(c % n * rep_size + home) * 2 + k] + s * count
            row = lax.div(place, LANES)
            w = k * every + c
            window[w : w + 1, 0:LANES] = noise[pl.ds(row, 1), :]
            after = jnp.minimum(row + 1, noise.shape[0] - 1)
            window[w : w + 1, LANES:] = noise[pl.ds(after, 1), :]
            low = jnp.where(number == w, lax.rem(place, LANES), low)
    seen = window[...]
    amount = 1
    while amount < LANES:
        turned = jnp.concatenate([seen[:, amount:], seen[:, :amount]], axis=1)
        seen = jnp.where(lax.rem(lax.div(low, amount), 2) == 1, turned, seen)
        amount *= 2
    window[...] = seen

    ybuf[...] = jnp.zeros_like(ybuf)
    fpad[...] = jnp.zeros_like(fpad)
    ebuf[...] = jnp.where(
        lax.broadcasted_iota(jnp.int32, (count, deep), 1) // GROUP
        == lax.broadcasted_iota(jnp.int32, (count, deep), 0), 1.0, 0.0
    ).astype(BF16)

    def pass_across(h):
        across_copies[h][0].start()
        for copy, forward in zip(mixed_copies[h], across_copies[h][1:]):
            copy.wait_recv()
            forward.start()

    tile = max(GROUP, min(deep, 262144 // wide) // GROUP * GROUP)
    share = tile // GROUP

    def bias_group(j):
        chol_copy(j).wait()
        first, tail, second = places[j]
        block_rows = mixbuf[:, :, first : first + GROUP, :].reshape(wide, width)
        if packed:
            ends = mixbuf[:, :, tail : tail + GROUP, :].reshape(wide, width)
            half = electrons - width
            ends = ends[:, half:] if second else ends[:, :half]
            block_rows = jnp.concatenate([block_rows, ends], axis=1)
        density = jnp.dot(block_rows, trial[...], preferred_element_type=F32).astype(BF16)

        @pl.loop(0, deep // tile)
        def _(t):
            block = cbuf[j, pl.ds(t * share, share)].reshape(tile, orbitals)
            at = pl.ds(pl.multiple_of(t * tile, tile), tile)
            ybuf[at, :] += lax.dot_general(block, density, NT, preferred_element_type=F32)

    pass_across(0)
    for copy in across_copies[0]:
        copy.wait_recv()
    loads[3].wait()
    for j in range(split - 1):
        bias_group(j)
    pass_across(1)
    bias_group(split - 1)
    for copy in across_copies[1]:
        copy.wait_recv()
    for j in range(split, groups):
        bias_group(j)

    same = (
        lax.broadcasted_iota(jnp.int32, (1, GROUP, wide), 1)
        == lax.broadcasted_iota(jnp.int32, (1, GROUP, wide), 2) % GROUP
    )
    traced = jnp.sum(jnp.where(same, ybuf[...].reshape(count, GROUP, wide), 0.0), axis=1)
    adder = jnp.where(
        lax.broadcasted_iota(jnp.int32, (walks, wide), 1) // GROUP
        == lax.broadcasted_iota(jnp.int32, (walks, wide), 0), 1.0, 0.0
    )
    partial = lax.dot_general(
        adder, traced, NT, preferred_element_type=F32, precision=lax.Precision.HIGHEST
    )
    fbsend[...] = partial
    fbbuf[me] = partial
    bias_copies = [remote(fbsend, fbbuf.at[me], fsem, (d,), holder(c)) for d, c in peers]
    for copy in bias_copies:
        copy.start()
    chain_step(1)
    for copy in pick_copies + bias_copies:
        copy.wait_recv()
    total = jnp.sum(fbbuf[...], axis=0)
    fpad[0:walks, :] = window[:, 0:LANES] - total
    fields = fpad[...].astype(BF16)

    some = min(16, walks)
    step = some * GROUP
    chunks = wide // step

    @pl.loop(0, chunks)
    def _(c):
        if chunks == 1:
            chosen = rbuf[...].reshape(step, LANES)
        else:
            per = every // some
            chosen = rbuf[c // per, pl.ds(lax.rem(c, per) * some, some)].reshape(step, LANES)
        spread = jnp.dot(chosen, fields, preferred_element_type=F32).astype(BF16)
        full = jnp.dot(spread, ebuf[...], preferred_element_type=F32)
        diagonal = (
            lax.broadcasted_iota(jnp.int32, (step, deep), 0) % GROUP
            == lax.broadcasted_iota(jnp.int32, (step, deep), 1) % GROUP
        )
        kron[c] = jnp.where(diagonal, full, 0.0).astype(BF16)

    def part_copy(j):
        return remote(psend.at[j], precv.at[j], qsem, (j,), sibling)

    def pot_copy(d, c, j):
        at = pl.ds(pl.multiple_of(j * GROUP, GROUP), GROUP)
        return remote(pfin.at[c, at], pot.at[a, q, at], psem, (d, j), holder(c))

    def finish(j):
        part_copy(j).wait_recv()
        at = pl.ds(pl.multiple_of(j * GROUP, GROUP), GROUP)
        pfin[:, at, :] = (field_scale * (keep[j] + precv[j].astype(F32))).astype(BF16)
        for d, b in peers:
            pot_copy(d, b, j).start()

    def potential_group(j):
        @pl.loop(0, chunks)
        def _(c):
            tmp[pl.ds(c * some, some)] = jnp.dot(
                kron[c], cbuf[j].reshape(deep, orbitals), preferred_element_type=F32
            ).reshape(some, GROUP, orbitals)

        psend[j] = tmp[pl.ds((1 - s) * every, every)].astype(BF16)
        part_copy(j).start()
        keep[j] = tmp[pl.ds(s * every, every)]

        @pl.when(j > 0)
        def _():
            finish(j - 1)

    pl.loop(0, groups)(potential_group)
    finish(groups - 1)
    if n > 2:
        chain_step(2)
    pot[a, q] = pfin[me]

    fbsend_rows = fpad.at[0:walks]
    fbsend_rows[...] = total
    for k in range(2):
        biasbuf[k : k + 1, :] = fpad[pl.ds(k * every + me, 1), :]
    bias_copy = pltpu.make_async_copy(biasbuf, bias_out, isem.at[4])
    bias_copy.start()

    for t in range(3, n):
        chain_step(t)
    xbuf[s] = wbuf[parents[s]]
    xsend[...] = wbuf[parents[1 - s]]
    child_copy = remote(xsend, xbuf.at[s], ssem, (1,), sibling)
    child_copy.start()
    child_copy.wait_recv()
    eye = jnp.where(
        lax.broadcasted_iota(jnp.int32, (electrons, electrons), 0)
        == lax.broadcasted_iota(jnp.int32, (electrons, electrons), 1), 1.0, 0.0
    ).astype(BF16)
    term = lax.dot_general(
        xbuf[...].reshape(electrons, orbitals), eye, (((0,), (0,)), ((), ())), preferred_element_type=F32
    ).astype(BF16)
    summed = term.astype(F32)

    @pl.loop(0, groups)
    def _(j):
        for d, b in peers:
            pot_copy(d, b, j).wait_recv()

    for degree in range(1, TAYLOR + 1):
        product = jnp.dot(
            pot[...].reshape(n * padded, orbitals), term, preferred_element_type=F32
        )
        term = (product * jnp.float32(1.0 / degree)).astype(BF16)
        if padded != rows:
            term = jnp.dot(layout, term, preferred_element_type=F32).astype(BF16)
        summed = summed + term.astype(F32)
    done[...] = lax.dot_general(
        eye, summed.astype(BF16), NT, preferred_element_type=F32
    ).astype(BF16).reshape(done.shape)
    last_copy = remote(done.at[1 - s], walkers_out.at[s], ssem, (2,), sibling)
    last_copy.start()
    kept_copy = pltpu.make_async_copy(done.at[s], walkers_out.at[s], isem.at[5])
    kept_copy.start()

    first_copy.wait_send()
    child_copy.wait_send()
    for copy in mixed_copies[0] + mixed_copies[1] + across_copies[0] + across_copies[1]:
        copy.wait_send()
    for copy in pick_copies + bias_copies:
        copy.wait_send()
    for t in range(n - 1):
        for way in range(2):
            @pl.when(chain_sends(way, t))
            def _():
                chain_copy(way, t).wait_send()

    @pl.loop(0, groups)
    def _(j):
        part_copy(j).wait_send()
        for d, b in peers:
            pot_copy(d, b, j).wait_send()

    bias_copy.wait()
    kept_copy.wait()
    last_copy.wait()


def hand_over(walkers, bias, walkers_out, bias_out):
    walkers_out[...] = walkers[...]
    bias_out[...] = bias[...]


def shards(cholesky, trial_orbitals, walkers, intersection_inverse, noise_stream, offsets, parents):
    count, rows, orbitals = cholesky.shape
    walk_count, _, half = walkers.shape
    electrons = trial_orbitals.shape[1]
    n = lax.axis_size("pair")
    assert walk_count == 2 and lax.axis_size("sub") == 2 and count == LANES
    ways = lax.axis_size("rep")
    if walk_count * n * ways * GROUP > 1024:
        ways = 1
    every = n * ways
    groups = -(-rows // (GROUP * ways))
    span = groups * GROUP
    padded = span * ways
    walks = walk_count * every
    _, _, sent, _, width = mixed_rows(groups, electrons)
    wide, deep = walks * GROUP, count * GROUP
    if padded != rows:
        cholesky = jnp.pad(cholesky, ((0, 0), (0, padded - rows), (0, 0)))

    vmem = pl.BlockSpec(memory_space=pltpu.VMEM)
    smem = pl.BlockSpec(memory_space=pltpu.SMEM)
    hbm = pl.BlockSpec(memory_space=pl.ANY)
    dma = pltpu.SemaphoreType.DMA
    new_walkers, force_bias = pl.pallas_call(
        functools.partial(step_kernel, n, ways, rows),
        out_shape=(
            jax.ShapeDtypeStruct((walk_count, half, orbitals), BF16),
            jax.ShapeDtypeStruct((walk_count, count), F32),
        ),
        in_specs=[hbm, hbm, hbm, hbm, hbm, smem, smem],
        out_specs=(hbm, hbm),
        scratch_shapes=[
            pltpu.VMEM((groups, count, GROUP, orbitals), BF16),
            pltpu.VMEM((2, half, orbitals), BF16),
            pltpu.VMEM((n, ways, sent, width), BF16),
            pltpu.VMEM((2, every, sent, width), BF16),
            pltpu.VMEM((walk_count * n, half, orbitals), BF16),
            pltpu.VMEM((2, every, GROUP, LANES), BF16),
            pltpu.VMEM((deep, wide), F32),
            pltpu.VMEM((count, deep), BF16),
            pltpu.VMEM((walks, count), F32),
            pltpu.VMEM((every, walks, count), F32),
            pltpu.VMEM((LANES, count), F32),
            pltpu.VMEM((walks // min(16, walks), min(16, walks) * GROUP, deep), BF16),
            pltpu.VMEM((walks, GROUP, orbitals), F32),
            pltpu.VMEM((groups, every, GROUP, orbitals), F32),
            pltpu.VMEM((groups, every, GROUP, orbitals), BF16),
            pltpu.VMEM((groups, every, GROUP, orbitals), BF16),
            pltpu.VMEM((every, span, orbitals), BF16),
            pltpu.VMEM((n, ways, span, orbitals), BF16),
            pltpu.VMEM((2, half, orbitals), BF16),
            pltpu.VMEM((half, orbitals), BF16),
            pltpu.VMEM((2, half, orbitals), BF16),
            pltpu.VMEM((walk_count, GROUP, LANES), BF16),
            pltpu.VMEM((walks, 2 * LANES), F32),
            pltpu.VMEM((electrons, orbitals), BF16),
            pltpu.VMEM((walk_count, electrons, electrons), BF16),
            pltpu.VMEM((noise_stream.shape[0] // LANES, LANES), F32),
            pltpu.VMEM((walk_count, count), F32),
            dma((groups,)),
            dma((2, 3)),
            dma((2, 2, every)),
            dma((2, 2, every)),
            dma((2, 2, n)),
            dma((2, every)),
            dma((2, every)),
            dma((2, groups)),
            dma((2, every, groups)),
            dma((6,)),
        ],
        compiler_params=pltpu.CompilerParams(
            collective_id=0, has_side_effects=True, vmem_limit_bytes=58 * 1024 * 1024
        ),
    )(
        cholesky, trial_orbitals.T, intersection_inverse, jnp.swapaxes(walkers, 1, 2),
        noise_stream.reshape(-1, LANES), offsets, parents,
    )
    new_walkers, force_bias = pl.pallas_call(
        hand_over,
        out_shape=(
            jax.ShapeDtypeStruct(new_walkers.shape, BF16),
            jax.ShapeDtypeStruct(force_bias.shape, F32),
        ),
        in_specs=[vmem, vmem],
        out_specs=(vmem, vmem),
        compiler_params=pltpu.CompilerParams(vmem_limit_bytes=58 * 1024 * 1024),
    )(new_walkers, force_bias)
    return (jnp.swapaxes(new_walkers, 1, 2), force_bias)


def solution(mesh):
    in_specs = (
        P("sub", "pair", None),
        P(),
        P(("grp", "pair", "rep"), None, "sub"),
        P(("grp", "pair", "rep"), None, None),
        P("grp"),
        P("grp"),
        P(("grp", "pair", "rep")),
    )
    out_specs = (P(("grp", "pair", "rep"), None, "sub"), P(("grp", "pair", "rep"), "sub"))
    return jax.shard_map(shards, mesh=mesh, in_specs=in_specs, out_specs=out_specs, check_vma=False)
```

```python
import functools

import jax
import jax.numpy as jnp
from jax import lax
from jax.experimental import pallas as pl
from jax.experimental.pallas import tpu as pltpu
from jax.sharding import PartitionSpec as P

TAYLOR = 6
GROUP = 16
LANES = 128

field_scale = 1.6

MESH = pl.DeviceIdType.MESH
F32 = jnp.float32
BF16 = jnp.bfloat16
NT = (((1,), (1,)), ((), ()))


def mixed_rows(groups, electrons):
    split = max(1, groups // 2)
    packed = electrons == LANES + LANES // 2
    places, row, starts = [], 0, []
    for low, high in ((0, split), (split, groups)):
        starts.append(row)
        tails = row + (high - low) * GROUP
        for i in range(high - low):
            places.append((row + i * GROUP, tails + i // 2 * GROUP, i % 2))
        row = tails + (-(-(high - low) // 2) * GROUP if packed else 0)
    return places, starts[1], row, packed, LANES if packed else electrons


def step_kernel(
    n, ways, rows, chol, trial_in, inverse_in, walkers_in, noise_in, offsets, parents,
    walkers_out, bias_out,
    cbuf, wfirst, mixed, mixbuf, wbuf, rbuf, ybuf, ebuf, fbsend, fbbuf, fpad, kron, tmp, keep, psend, precv,
    pfin, pot, xbuf, xsend, done, picks, window, trial, inverse, noise, biasbuf,
    csem, ssem, msem, xsem, hsem, rsem, fsem, qsem, psem, isem,
):
    a = lax.axis_index("pair")
    s = lax.axis_index("sub")
    groups, count = cbuf.shape[0], cbuf.shape[1]
    electrons, orbitals = trial.shape
    every = n * ways
    q = lax.axis_index("rep") if ways > 1 else 0
    me = q * n + a
    span = groups * GROUP
    padded = span * ways
    walks = 2 * every
    wide = walks * GROUP
    deep = count * GROUP

    def chol_copy(j):
        return pltpu.make_async_copy(
            chol.at[:, pl.ds(pl.multiple_of(q * span + j * GROUP, GROUP), GROUP), :],
            cbuf.at[j], csem.at[j],
        )

    own_walkers = pl.ds(2 * a, 2)
    loads = [
        pltpu.make_async_copy(src, dst, isem.at[i])
        for i, (src, dst) in enumerate(
            [(walkers_in, wbuf.at[own_walkers]), (inverse_in, inverse), (noise_in, noise), (trial_in, trial)]
        )
    ]
    for load in loads:
        load.start()

    @pl.loop(0, groups)
    def _(j):
        chol_copy(j).start()

    peers = [(d, lax.rem(me + d, every)) for d in range(1, every)]

    def holder(c):
        return {"pair": lax.rem(c, n), "rep": lax.div(c, n)} if ways > 1 else {"pair": c}
    sibling = {"sub": 1 - s}

    def remote(src, dst, sems, place, target):
        return pltpu.make_async_remote_copy(
            src_ref=src, dst_ref=dst, send_sem=sems.at[(0,) + place], recv_sem=sems.at[(1,) + place],
            device_id=target, device_id_type=MESH,
        )

    spots = lax.broadcasted_iota(jnp.int32, (GROUP, LANES), 1)
    for k in range(2):
        column = lax.rem(parents[k], 2) * every + q * n + lax.div(parents[k], 2)
        picks[k] = jnp.where(spots == column, 1.0, 0.0).astype(BF16)

    barrier = pltpu.get_barrier_semaphore()
    pl.semaphore_signal(barrier, inc=1, device_id=sibling, device_id_type=MESH)
    for _, c in peers:
        pl.semaphore_signal(barrier, inc=1, device_id=holder(c), device_id_type=MESH)
    loads[0].wait()
    pl.semaphore_wait(barrier, every)

    first_copy = remote(wbuf.at[2 * a + 1 - s], wfirst.at[s], ssem, (0,), sibling)
    first_copy.start()
    pick_copies = [remote(picks, rbuf.at[:, me], rsem, (d,), holder(c)) for d, c in peers]
    for copy in pick_copies:
        copy.start()
    wfirst[s] = wbuf[2 * a + s]
    rbuf[:, me] = picks[...]
    loads[1].wait()
    loads[2].wait()
    if padded != rows:
        spot = lax.broadcasted_iota(jnp.int32, (orbitals, n * padded), 1)
        spot = jnp.where(spot % padded < rows, spot // padded * rows + spot % padded, -1)
        layout = jnp.where(
            spot == lax.broadcasted_iota(jnp.int32, (orbitals, n * padded), 0), 1.0, 0.0
        ).astype(BF16)
    first_copy.wait_recv()
    start = wfirst[...].reshape(electrons, orbitals)
    if padded != rows:
        start = jnp.dot(start, layout, preferred_element_type=F32).astype(BF16)
    product = lax.dot_general(
        start, inverse[s], (((0,), (0,)), ((), ())), preferred_element_type=F32
    ).astype(BF16).reshape(n, ways, span, electrons)
    places, cut, sent, packed, width = mixed_rows(groups, electrons)
    for j, (first, tail, second) in enumerate(places):
        rows_of = product[:, :, j * GROUP : (j + 1) * GROUP, :]
        mixed[:, :, first : first + GROUP, :] = rows_of[..., :width]
        if packed and not second:
            beside = (
                product[:, :, (j + 1) * GROUP : (j + 2) * GROUP, width:]
                if j + 1 < groups and places[j + 1][2]
                else jnp.zeros_like(rows_of[..., width:])
            )
            mixed[:, :, tail : tail + GROUP, :] = jnp.concatenate([rows_of[..., width:], beside], axis=-1)

    def chain_copy(way, t):
        block = a - t if way == 0 else a + t
        at = pl.ds(2 * block, 2)
        return remote(wbuf.at[at], wbuf.at[at], hsem, (way, t), {"pair": a + 1 - 2 * way})

    def chain_sends(way, t):
        return (a >= t) & (a + 1 < n) if way == 0 else (a + t < n) & (a > 0)

    def chain_gets(way, t):
        return a >= t + 1 if way == 0 else a + t + 1 < n

    def chain_step(t):
        for way in range(2):
            if t > 0:
                @pl.when(chain_gets(way, t - 1))
                def _():
                    back = a - t if way == 0 else a + t
                    at = pl.ds(2 * back, 2)
                    remote(
                        wbuf.at[at], wbuf.at[at], hsem, (way, t - 1), {"pair": a - 1 + 2 * way}
                    ).wait_recv()
            if t < n - 1:
                @pl.when(chain_sends(way, t))
                def _():
                    chain_copy(way, t).start()

    split = max(1, groups // 2)
    parts = [pl.ds(0, cut), pl.ds(cut, sent - cut)]
    mixed_copies = [
        [
            remote(
                mixed.at[lax.rem(c, n), lax.div(c, n), part], mixbuf.at[s, me, part], msem, (h, d), holder(c)
            )
            for d, c in peers
        ]
        for h, part in enumerate(parts)
    ]
    across_copies = [
        [
            remote(mixbuf.at[s, c, part], mixbuf.at[s, c, part], xsem, (h, d), sibling)
            for d, c in [(d, lax.rem(me + every - d, every)) for d in range(every)]
        ]
        for h, part in enumerate(parts)
    ]
    for h in range(2):
        for copy in mixed_copies[h]:
            copy.start()
    chain_step(0)
    mixbuf[s, me] = mixed[a, q]

    rep, rep_size = lax.axis_index("rep"), lax.axis_size("rep")
    low = jnp.zeros((walks, 2 * LANES), jnp.int32)
    number = lax.broadcasted_iota(jnp.int32, (walks, 2 * LANES), 0)
    for c in range(every):
        for k in range(2):
            home = c // n if ways > 1 else rep
            place = offsets[(c % n * rep_size + home) * 2 + k] + s * count
            row = lax.div(place, LANES)
            w = k * every + c
            window[w : w + 1, 0:LANES] = noise[pl.ds(row, 1), :]
            after = jnp.minimum(row + 1, noise.shape[0] - 1)
            window[w : w + 1, LANES:] = noise[pl.ds(after, 1), :]
            low = jnp.where(number == w, lax.rem(place, LANES), low)
    seen = window[...]
    amount = 1
    while amount < LANES:
        turned = jnp.concatenate([seen[:, amount:], seen[:, :amount]], axis=1)
        seen = jnp.where(lax.rem(lax.div(low, amount), 2) == 1, turned, seen)
        amount *= 2
    window[...] = seen

    ybuf[...] = jnp.zeros_like(ybuf)
    fpad[...] = jnp.zeros_like(fpad)
    ebuf[...] = jnp.where(
        lax.broadcasted_iota(jnp.int32, (count, deep), 1) // GROUP
        == lax.broadcasted_iota(jnp.int32, (count, deep), 0), 1.0, 0.0
    ).astype(BF16)

    def pass_across(h):
        across_copies[h][0].start()
        for copy, forward in zip(mixed_copies[h], across_copies[h][1:]):
            copy.wait_recv()
            forward.start()

    tile = max(GROUP, min(deep, 262144 // wide) // GROUP * GROUP)
    share = tile // GROUP

    def bias_group(j):
        chol_copy(j).wait()
        first, tail, second = places[j]
        block_rows = mixbuf[:, :, first : first + GROUP, :].reshape(wide, width)
        if packed:
            ends = mixbuf[:, :, tail : tail + GROUP, :].reshape(wide, width)
            half = electrons - width
            ends = ends[:, half:] if second else ends[:, :half]
            block_rows = jnp.concatenate([block_rows, ends], axis=1)
        density = jnp.dot(block_rows, trial[...], preferred_element_type=F32).astype(BF16)

        @pl.loop(0, deep // tile)
        def _(t):
            block = cbuf[j, pl.ds(t * share, share)].reshape(tile, orbitals)
            at = pl.ds(pl.multiple_of(t * tile, tile), tile)
            ybuf[at, :] += lax.dot_general(block, density, NT, preferred_element_type=F32)

    pass_across(0)
    for copy in across_copies[0]:
        copy.wait_recv()
    loads[3].wait()
    for j in range(split - 1):
        bias_group(j)
    pass_across(1)
    bias_group(split - 1)
    for copy in across_copies[1]:
        copy.wait_recv()
    for j in range(split, groups):
        bias_group(j)

    same = (
        lax.broadcasted_iota(jnp.int32, (1, GROUP, wide), 1)
        == lax.broadcasted_iota(jnp.int32, (1, GROUP, wide), 2) % GROUP
    )
    traced = jnp.sum(jnp.where(same, ybuf[...].reshape(count, GROUP, wide), 0.0), axis=1)
    adder = jnp.where(
        lax.broadcasted_iota(jnp.int32, (walks, wide), 1) // GROUP
        == lax.broadcasted_iota(jnp.int32, (walks, wide), 0), 1.0, 0.0
    )
    partial = lax.dot_general(
        adder, traced, NT, preferred_element_type=F32, precision=lax.Precision.HIGHEST
    )
    fbsend[...] = partial
    fbbuf[me] = partial
    bias_copies = [remote(fbsend, fbbuf.at[me], fsem, (d,), holder(c)) for d, c in peers]
    for copy in bias_copies:
        copy.start()
    for copy in pick_copies + bias_copies:
        copy.wait_recv()
    chain_step(1)
    total = jnp.sum(fbbuf[...], axis=0)
    fpad[0:walks, :] = window[:, 0:LANES] - total
    fields = fpad[...].astype(BF16)

    some = min(16, walks)
    step = some * GROUP
    chunks = wide // step

    @pl.loop(0, chunks)
    def _(c):
        if chunks == 1:
            chosen = rbuf[...].reshape(step, LANES)
        else:
            per = every // some
            chosen = rbuf[c // per, pl.ds(lax.rem(c, per) * some, some)].reshape(step, LANES)
        spread = jnp.dot(chosen, fields, preferred_element_type=F32).astype(BF16)
        full = jnp.dot(spread, ebuf[...], preferred_element_type=F32)
        diagonal = (
            lax.broadcasted_iota(jnp.int32, (step, deep), 0) % GROUP
            == lax.broadcasted_iota(jnp.int32, (step, deep), 1) % GROUP
        )
        kron[c] = jnp.where(diagonal, full, 0.0).astype(BF16)

    def part_copy(j):
        return remote(psend.at[j], precv.at[j], qsem, (j,), sibling)

    def pot_copy(d, c, j):
        at = pl.ds(pl.multiple_of(j * GROUP, GROUP), GROUP)
        return remote(pfin.at[c, at], pot.at[a, q, at], psem, (d, j), holder(c))

    def finish(j):
        part_copy(j).wait_recv()
        at = pl.ds(pl.multiple_of(j * GROUP, GROUP), GROUP)
        pfin[:, at, :] = (field_scale * (keep[j] + precv[j].astype(F32))).astype(BF16)
        for d, b in peers:
            pot_copy(d, b, j).start()

    def potential_group(j):
        @pl.loop(0, chunks)
        def _(c):
            tmp[pl.ds(c * some, some)] = jnp.dot(
                kron[c], cbuf[j].reshape(deep, orbitals), preferred_element_type=F32
            ).reshape(some, GROUP, orbitals)

        psend[j] = tmp[pl.ds((1 - s) * every, every)].astype(BF16)
        part_copy(j).start()
        keep[j] = tmp[pl.ds(s * every, every)]

        @pl.when(j > 0)
        def _():
            finish(j - 1)

    pl.loop(0, groups)(potential_group)
    finish(groups - 1)
    if n > 2:
        chain_step(2)
    pot[a, q] = pfin[me]

    fbsend_rows = fpad.at[0:walks]
    fbsend_rows[...] = total
    for k in range(2):
        biasbuf[k : k + 1, :] = fpad[pl.ds(k * every + me, 1), :]
    bias_copy = pltpu.make_async_copy(biasbuf, bias_out, isem.at[4])
    bias_copy.start()

    for t in range(3, n):
        chain_step(t)
    xbuf[s] = wbuf[parents[s]]
    xsend[...] = wbuf[parents[1 - s]]
    child_copy = remote(xsend, xbuf.at[s], ssem, (1,), sibling)
    child_copy.start()
    child_copy.wait_recv()
    eye = jnp.where(
        lax.broadcasted_iota(jnp.int32, (electrons, electrons), 0)
        == lax.broadcasted_iota(jnp.int32, (electrons, electrons), 1), 1.0, 0.0
    ).astype(BF16)
    term = lax.dot_general(
        xbuf[...].reshape(electrons, orbitals), eye, (((0,), (0,)), ((), ())), preferred_element_type=F32
    ).astype(BF16)
    summed = term.astype(F32)

    @pl.loop(0, groups)
    def _(j):
        for d, b in peers:
            pot_copy(d, b, j).wait_recv()

    for degree in range(1, TAYLOR + 1):
        product = jnp.dot(
            pot[...].reshape(n * padded, orbitals), term, preferred_element_type=F32
        )
        term = (product * jnp.float32(1.0 / degree)).astype(BF16)
        if padded != rows:
            term = jnp.dot(layout, term, preferred_element_type=F32).astype(BF16)
        summed = summed + term.astype(F32)
    done[...] = lax.dot_general(
        eye, summed.astype(BF16), NT, preferred_element_type=F32
    ).astype(BF16).reshape(done.shape)
    last_copy = remote(done.at[1 - s], walkers_out.at[s], ssem, (2,), sibling)
    last_copy.start()
    kept_copy = pltpu.make_async_copy(done.at[s], walkers_out.at[s], isem.at[5])
    kept_copy.start()

    first_copy.wait_send()
    child_copy.wait_send()
    for copy in mixed_copies[0] + mixed_copies[1] + across_copies[0] + across_copies[1]:
        copy.wait_send()
    for copy in pick_copies + bias_copies:
        copy.wait_send()
    for t in range(n - 1):
        for way in range(2):
            @pl.when(chain_sends(way, t))
            def _():
                chain_copy(way, t).wait_send()

    @pl.loop(0, groups)
    def _(j):
        part_copy(j).wait_send()
        for d, b in peers:
            pot_copy(d, b, j).wait_send()

    bias_copy.wait()
    kept_copy.wait()
    last_copy.wait()


def hand_over(walkers, bias, walkers_out, bias_out):
    walkers_out[...] = walkers[...]
    bias_out[...] = bias[...]


def shards(cholesky, trial_orbitals, walkers, intersection_inverse, noise_stream, offsets, parents):
    count, rows, orbitals = cholesky.shape
    walk_count, _, half = walkers.shape
    electrons = trial_orbitals.shape[1]
    n = lax.axis_size("pair")
    assert walk_count == 2 and lax.axis_size("sub") == 2 and count == LANES
    ways = lax.axis_size("rep")
    if walk_count * n * ways * GROUP > 1024:
        ways = 1
    every = n * ways
    groups = -(-rows // (GROUP * ways))
    span = groups * GROUP
    padded = span * ways
    walks = walk_count * every
    _, _, sent, _, width = mixed_rows(groups, electrons)
    wide, deep = walks * GROUP, count * GROUP
    if padded != rows:
        cholesky = jnp.pad(cholesky, ((0, 0), (0, padded - rows), (0, 0)))

    vmem = pl.BlockSpec(memory_space=pltpu.VMEM)
    smem = pl.BlockSpec(memory_space=pltpu.SMEM)
    hbm = pl.BlockSpec(memory_space=pl.ANY)
    dma = pltpu.SemaphoreType.DMA
    new_walkers, force_bias = pl.pallas_call(
        functools.partial(step_kernel, n, ways, rows),
        out_shape=(
            jax.ShapeDtypeStruct((walk_count, half, orbitals), BF16),
            jax.ShapeDtypeStruct((walk_count, count), F32),
        ),
        in_specs=[hbm, hbm, hbm, hbm, hbm, smem, smem],
        out_specs=(hbm, hbm),
        scratch_shapes=[
            pltpu.VMEM((groups, count, GROUP, orbitals), BF16),
            pltpu.VMEM((2, half, orbitals), BF16),
            pltpu.VMEM((n, ways, sent, width), BF16),
            pltpu.VMEM((2, every, sent, width), BF16),
            pltpu.VMEM((walk_count * n, half, orbitals), BF16),
            pltpu.VMEM((2, every, GROUP, LANES), BF16),
            pltpu.VMEM((deep, wide), F32),
            pltpu.VMEM((count, deep), BF16),
            pltpu.VMEM((walks, count), F32),
            pltpu.VMEM((every, walks, count), F32),
            pltpu.VMEM((LANES, count), F32),
            pltpu.VMEM((walks // min(16, walks), min(16, walks) * GROUP, deep), BF16),
            pltpu.VMEM((walks, GROUP, orbitals), F32),
            pltpu.VMEM((groups, every, GROUP, orbitals), F32),
            pltpu.VMEM((groups, every, GROUP, orbitals), BF16),
            pltpu.VMEM((groups, every, GROUP, orbitals), BF16),
            pltpu.VMEM((every, span, orbitals), BF16),
            pltpu.VMEM((n, ways, span, orbitals), BF16),
            pltpu.VMEM((2, half, orbitals), BF16),
            pltpu.VMEM((half, orbitals), BF16),
            pltpu.VMEM((2, half, orbitals), BF16),
            pltpu.VMEM((walk_count, GROUP, LANES), BF16),
            pltpu.VMEM((walks, 2 * LANES), F32),
            pltpu.VMEM((electrons, orbitals), BF16),
            pltpu.VMEM((walk_count, electrons, electrons), BF16),
            pltpu.VMEM((noise_stream.shape[0] // LANES, LANES), F32),
            pltpu.VMEM((walk_count, count), F32),
            dma((groups,)),
            dma((2, 3)),
            dma((2, 2, every)),
            dma((2, 2, every)),
            dma((2, 2, n)),
            dma((2, every)),
            dma((2, every)),
            dma((2, groups)),
            dma((2, every, groups)),
            dma((6,)),
        ],
        compiler_params=pltpu.CompilerParams(
            collective_id=0, has_side_effects=True, vmem_limit_bytes=58 * 1024 * 1024
        ),
    )(
        cholesky, trial_orbitals.T, intersection_inverse, jnp.swapaxes(walkers, 1, 2),
        noise_stream.reshape(-1, LANES), offsets, parents,
    )
    new_walkers, force_bias = pl.pallas_call(
        hand_over,
        out_shape=(
            jax.ShapeDtypeStruct(new_walkers.shape, BF16),
            jax.ShapeDtypeStruct(force_bias.shape, F32),
        ),
        in_specs=[vmem, vmem],
        out_specs=(vmem, vmem),
        compiler_params=pltpu.CompilerParams(vmem_limit_bytes=58 * 1024 * 1024),
    )(new_walkers, force_bias)
    return (jnp.swapaxes(new_walkers, 1, 2), force_bias)


def solution(mesh):
    in_specs = (
        P("sub", "pair", None),
        P(),
        P(("grp", "pair", "rep"), None, "sub"),
        P(("grp", "pair", "rep"), None, None),
        P("grp"),
        P("grp"),
        P(("grp", "pair", "rep")),
    )
    out_specs = (P(("grp", "pair", "rep"), None, "sub"), P(("grp", "pair", "rep"), "sub"))
    return jax.shard_map(shards, mesh=mesh, in_specs=in_specs, out_specs=out_specs, check_vma=False)
```
